128 devices in a mesh: gx: 4 (over y), gy: 4 (over z_lo, core), gz: 8 (over z_hi, x).
Axes of the slice: x: 4, y: 4, z: 4 (z_hi: 2, z_lo: 2; z = z_hi * 2 + z_lo), core: 2. Of those that a mesh axis runs over, the one named last changes fastest.
Arguments:
- density: bfloat16 [256, 512, 512], P('gz', 'gx', 'gy'), as said below
Outputs:
- potential: float32 [256, 512, 512], P('gz', 'gx', 'gy')
- acceleration: bfloat16 [3, 256, 512, 512], P(None, 'gz', 'gx', 'gy')
Inputs may be any that keep to these rules, and one draw needn't show every extreme that they name: `density`: every cell's mass is positive.
All inputs are finite; a program needn't handle non-finite values.
Results may differ from the reference program's by a relative error of at most 0.0025.
Values sent between devices are 32-bit elements; how exact they have to be, the bound alone decides.
No kernel may reach another device: no remote copies, remote signals or barrier semaphores. Data moves between devices by JAX's collectives and lax.ppermute only.
A program may use at most 192 MiB of HBM per device.

```python
import math
import jax
import jax.numpy as jnp
from jax import lax

HOCK = 72
RATIO = 4
PATCH = 32
CQ = 8
CNX = 128
CNY = 128
CNZ = 64
NZ = 256
NX = 512
NY = 512


def draw_density(key, part):
    key = jax.random.fold_in(key, 11)
    noise = jax.random.normal(key, (NZ, NX, NY), jnp.float32)
    values = jnp.exp(0.693147 * jnp.clip(noise, -4.0, 4.0))
    return values.astype(jnp.bfloat16)


def setup_inputs(seed: int = 0) -> dict:
    streams_of = jax.random.split(jax.random.key(seed), 2)
    return {
        "density": draw_density(jax.random.fold_in(streams_of[1], 71), 0),
    }


highest = lax.Precision.HIGHEST

def green_cube(length):
    index = jnp.arange(length, dtype=jnp.int32)
    offset = jnp.minimum(index, length - index).astype(jnp.float32)
    square = offset[:, None, None] ** 2 + offset[None, :, None] ** 2 + offset[None, None, :] ** 2
    radius = jnp.sqrt(jnp.maximum(square, 1.0))
    return jnp.where(square > 0.0, 1.0 / (4.0 * math.pi * radius), 0.25)

def coarse_table(cells, ratio):
    source = jnp.arange(cells, dtype=jnp.int32) + 2
    target = jnp.arange(cells + 4, dtype=jnp.int32)
    apart = (target[None, :] - source[:, None]).astype(jnp.float32)
    sq_apart = apart ** 2
    square = sq_apart[:, None, None, :, None, None] + sq_apart[None, :, None, None, :, None] + sq_apart[None, None, :, None, None, :]
    radius = jnp.sqrt(jnp.maximum(square, 1.0))
    table = jnp.where(square > 0.0, 1.0 / (4.0 * math.pi * ratio * radius), 0.25 / ratio)
    return table.reshape(cells ** 3, (cells + 4) ** 3)

def refine(coarse_ext, axis, ratio):
    inner = coarse_ext.shape[axis] - 2
    shifted = [lax.slice_in_dim(coarse_ext, offset, offset + inner, axis=axis) for offset in range(3)]
    layers = []
    for within in range(ratio):
        place = (within + 0.5) / ratio + 0.5
        weights = [max(0.0, 1.0 - abs(place - offset)) for offset in range(3)]
        layers.append(weights[0] * shifted[0] + weights[1] * shifted[1] + weights[2] * shifted[2])
    stacked = jnp.stack(layers, axis=axis + 1)
    new_shape = list(coarse_ext.shape)
    new_shape[axis] = inner * ratio
    return stacked.reshape(new_shape)

def pad_along(values, axis, low, high):
    widths = [(0, 0)] * values.ndim
    widths[axis] = (low, high)
    return jnp.pad(values, widths)

def intersection_add(values, axis, span):
    count = values.shape[axis]
    width = values.shape[axis + 1]
    extra = width - span
    shape = list(values.shape)
    main = lax.slice_in_dim(values, 0, span, axis=axis + 1)
    main = main.reshape(shape[:axis] + [count * span] + shape[axis + 2:])
    main = pad_along(main, axis, 0, extra)
    tail = lax.slice_in_dim(values, span, width, axis=axis + 1)
    tail = pad_along(pad_along(tail, axis + 1, 0, span - extra), axis, 1, 0)
    tail = tail.reshape(shape[:axis] + [(count + 1) * span] + shape[axis + 2:])
    tail = lax.slice_in_dim(tail, 0, count * span + extra, axis=axis)
    return main + tail

def wrap_fold(values, axis, margin, length):
    middle = lax.slice_in_dim(values, margin, margin + length, axis=axis)
    beyond = lax.slice_in_dim(values, margin + length, 2 * margin + length, axis=axis)
    before = lax.slice_in_dim(values, 0, margin, axis=axis)
    return middle + pad_along(beyond, axis, 0, length - margin) + pad_along(before, axis, length - margin, 0)

def lattice_eigen(freq, length):
    return 2.0 - 2.0 * jnp.cos((freq % length).astype(jnp.float32) * (2.0 * math.pi / length))

def reference(density):
    margin = RATIO
    region = PATCH + 2 * margin
    count_z, count_x, count_y = (CNZ // CQ, CNX // CQ, CNY // CQ)
    masses = density.astype(jnp.float32).reshape(CNZ, RATIO, CNX, RATIO, CNY, RATIO).sum(axis=(1, 3, 5))
    blocks = masses.reshape(count_z, CQ, count_x, CQ, count_y, CQ).transpose(0, 2, 4, 1, 3, 5)
    local_coarse = jnp.dot(blocks.reshape(-1, CQ ** 3), coarse_table(CQ, RATIO), precision=highest, preferred_element_type=jnp.float32)
    local_coarse = local_coarse.reshape(count_z, count_x, count_y, CQ + 4, CQ + 4, CQ + 4)
    green_hat = jnp.fft.rfftn(green_cube(HOCK))
    zero_index = jnp.zeros((), jnp.int32)
    after = HOCK - PATCH - margin

    def slab_near(index, summed):
        row_z = (index // count_x).astype(jnp.int32)
        row_x = (index % count_x).astype(jnp.int32)
        slab = lax.dynamic_slice(density, (row_z * PATCH, row_x * PATCH, zero_index), (PATCH, PATCH, NY)).astype(jnp.float32)
        cubes = slab.reshape(PATCH, PATCH, count_y, PATCH).transpose(2, 0, 1, 3)
        padded = jnp.pad(cubes, ((0, 0), (margin, after), (margin, after), (margin, after)))
        spectra = jnp.fft.rfftn(padded, axes=(1, 2, 3)) * green_hat[None]
        field = jnp.fft.irfftn(spectra, s=(HOCK, HOCK, HOCK), axes=(1, 2, 3))
        field = field[:, :region, :region, :region].astype(jnp.float32)
        windows = local_coarse[row_z, row_x]
        smooth = refine(refine(refine(windows, 1, RATIO), 2, RATIO), 3, RATIO)
        part = (field - smooth).transpose(1, 2, 0, 3)
        part = intersection_add(part, 2, PATCH)
        start = (row_z * PATCH, row_x * PATCH, zero_index)
        old = lax.dynamic_slice(summed, start, (region, region, NY + 2 * margin))
        return lax.dynamic_update_slice(summed, old + part, start)
    summed = jnp.zeros((NZ + 2 * margin, NX + 2 * margin, NY + 2 * margin), jnp.float32)
    summed = lax.fori_loop(0, count_z * count_x, slab_near, summed)
    near_all = wrap_fold(summed, 0, margin, NZ)
    near_all = wrap_fold(near_all, 1, margin, NX)
    near_all = wrap_fold(near_all, 2, margin, NY)
    freq_z = jnp.arange(CNZ, dtype=jnp.int32)
    freq_x = jnp.arange(CNX, dtype=jnp.int32)
    freq_y = jnp.arange(CNY, dtype=jnp.int32)
    eigen = lattice_eigen(freq_z, CNZ)[:, None, None] + lattice_eigen(freq_x, CNX)[None, :, None] + lattice_eigen(freq_y, CNY)[None, None, :]
    zero_mode = (freq_z == 0)[:, None, None] & (freq_x == 0)[None, :, None] & (freq_y == 0)[None, None, :]
    factor = jnp.where(zero_mode, 0.0, 1.0 / (RATIO * jnp.where(zero_mode, 1.0, eigen)))
    far = jnp.real(jnp.fft.ifftn(jnp.fft.fftn(masses) * factor)).astype(jnp.float32)
    far_ext = jnp.pad(far, 1, mode='wrap')
    far_fine = refine(refine(refine(far_ext, 0, RATIO), 1, RATIO), 2, RATIO)
    potential = near_all + far_fine

    def gradient(axis):
        ahead_one = jnp.roll(potential, -1, axis)
        behind_one = jnp.roll(potential, 1, axis)
        ahead_two = jnp.roll(potential, -2, axis)
        behind_two = jnp.roll(potential, 2, axis)
        value = -(2.0 / 3.0 * (ahead_one - behind_one) - 1.0 / 12.0 * (ahead_two - behind_two))
        return value.astype(jnp.bfloat16)
    acceleration = jnp.stack([gradient(0), gradient(1), gradient(2)])
    return (potential, acceleration)
```

```python
import functools
import math

import jax
import jax.numpy as jnp
import ml_dtypes
import numpy as np
from jax import lax
from jax.experimental import pallas as pl
from jax.experimental.pallas import tpu as pltpu
from jax.sharding import PartitionSpec as P

HOCK = 72
RATIO = 4
PATCH = 32
CQ = 8
CH = HOCK // RATIO
NF = HOCK // 2 + 1
NC = CH // 2 + 1
NG = 48
PAIRS = 320

f32 = jnp.float32
b16 = jnp.bfloat16
MIB = 1 << 20


def halves(table):
    high = table.astype(ml_dtypes.bfloat16)
    low = (table - high.astype(np.float64)).astype(ml_dtypes.bfloat16)
    return high, low


def centred(length, cells, centre):
    freq = np.arange(length // 2 + 1)
    weight = np.where((freq == 0) | (freq == length // 2), 1.0, 2.0)
    angle = 2.0 * math.pi / length * freq[:, None] * (cells - centre)[None, :]
    basis = np.stack([np.cos(angle), np.sin(angle)], axis=1)
    basis *= np.sqrt(weight / length)[:, None, None]
    return np.where(np.abs(basis) < 1e-12, 0.0, basis)


def fine_basis(cells):
    return centred(HOCK, cells, (PATCH - 1) / 2)


def coarse_basis(cells):
    return centred(CH, cells, (CQ - 1) / 2)


def inverse_distance(square, ratio):
    return np.where(
        square > 0, 1.0 / (4.0 * math.pi * ratio * np.sqrt(np.maximum(square, 1))), 0.25 / ratio
    )


def line_spectra(length, reach, ratio):
    index = np.arange(length)
    wrap = np.minimum(index, length - index)
    side = np.arange(reach)
    square = side[:, None, None] ** 2 + side[None, :, None] ** 2 + wrap[None, None, :] ** 2
    kernel = inverse_distance(square, ratio)
    cosine = np.cos(2.0 * math.pi / length * np.outer(np.arange(length // 2 + 1), index))
    return np.einsum("fd,abd->fab", cosine, kernel)


def refine_table(fine, coarse):
    return np.maximum(0.0, 1.0 - np.abs((fine[:, None] + 0.5) / RATIO - 0.5 - coarse[None, :]))


def sign(odd, mirrored):
    return -1.0 if (odd and mirrored) else 1.0


def dense_table():
    spectra = line_spectra(HOCK, 36, 1)
    target = np.arange(20)[:, None] - RATIO
    source = np.arange(16)[None, :]
    near, far = np.abs(target - source), np.abs(target - (PATCH - 1 - source))
    result = np.empty((NF, 4, 2, 400, 256), ml_dtypes.bfloat16)

    def pick(first, second):
        return spectra[:, first[:, None, :, None], second[None, :, None, :]]

    terms = {(a, b): pick((near, far)[a], (near, far)[b]) for a in (0, 1) for b in (0, 1)}
    for parity in range(4):
        odd_z, odd_x = divmod(parity, 2)
        total = sum(sign(odd_z, a) * sign(odd_x, b) * terms[a, b] for a in (0, 1) for b in (0, 1))
        high, low = halves(0.25 * total.reshape(NF, 400, 256))
        result[:, parity, 0], result[:, parity, 1] = high, low
    return result


def coarse_dense_table():
    spectra = line_spectra(CH, 10, RATIO)
    window = np.arange(-2, CQ + 2)
    apart = np.abs(window[:, None] - np.arange(CQ)[None, :])
    kernel = spectra[:, apart[:, None, :, None], apart[None, :, None, :]]
    spread = refine_table(np.arange(20) - RATIO, window)
    kernel = np.einsum("za,xb,fabcd->fcdzx", spread, spread, kernel)
    result = np.empty((NC, 4, 2, 16, 400), ml_dtypes.bfloat16)
    for parity in range(4):
        odd_z, odd_x = divmod(parity, 2)
        mirrored = kernel[:, ::-1]
        total = kernel + (-1.0) ** odd_z * mirrored
        total = total + (-1.0) ** odd_x * total[:, :, ::-1]
        total = 0.25 * total[:, :4, :4].reshape(NC, 16, 400)
        result[:, parity, 0], result[:, parity, 1] = halves(total)
    return result


def forward_table():
    cells = np.arange(PATCH)
    lines = np.zeros((NG, 2, PATCH))
    lines[:NF] = fine_basis(cells)
    lines[NF : NF + NC] = coarse_basis(cells // RATIO)
    table = np.zeros((NG, 4, 2, 4, 4, 4, PATCH))
    for parity in range(4):
        odd_z, odd_x = divmod(parity, 2)
        for mirror in range(4):
            mirror_z, mirror_x = divmod(mirror, 2)
            factor = sign(odd_z, mirror_z) * sign(odd_x, mirror_x)
            for patch in range(4):
                table[:, parity, :, patch, mirror, patch] = factor * lines
    high, low = halves(table.reshape(12, 128, 512))
    return np.concatenate([high, low], axis=1)


def mirror_table():
    table = np.zeros((64, 128))
    for patch in range(4):
        for cell in range(16):
            table[patch * 16 + cell, patch * 32 + 31 - cell] = 1.0
    return table.astype(ml_dtypes.bfloat16)


def gather_table():
    table = np.zeros((16, 16, 4, 4))
    for z in range(16):
        for x in range(16):
            table[z, x, z // RATIO, x // RATIO] = 1.0
    return table.reshape(256, 16).astype(ml_dtypes.bfloat16)


def alias_weights():
    fine = np.arange(HOCK)
    spread = np.zeros((HOCK, CH))
    for shift in (-1, 0, 1):
        spread += refine_table(fine, np.arange(CH) + shift * CH)
    mapped = np.einsum("fct,tY,GcY->fcG", fine_basis(fine), spread, coarse_basis(np.arange(CH)))
    rest = np.arange(NF) % CH
    alias = np.minimum(rest, CH - rest)
    return mapped[np.arange(NF), :, alias]


BLOCK = 128
BEYOND = [128, 129, 130, 131, -4, -3, -2, -1]
UPPER = [128, 129, 130, 131, 124, 125, 126, 127]
LOWER = [0, 1, 2, 3, -4, -3, -2, -1]
PLACES = np.array(list(range(BLOCK)) + BEYOND + UPPER + LOWER)


def backward_table():
    table = np.zeros((160, 38, 2, 4))
    for patch in range(4):
        cells = PLACES - PATCH * patch
        inside = (cells >= -RATIO) & (cells < PATCH + RATIO)
        values = fine_basis(cells) * inside
        table[:152, :NF, :, patch] = values.transpose(2, 0, 1)
    return np.stack(halves(table.reshape(160, 304)))


def unfold_table():
    table = np.zeros((2, 2, 160, 2, 4, 2, 20))
    for odd in range(2):
        for patch in range(4):
            for row, place in enumerate(PLACES):
                cell = place - PATCH * patch + RATIO
                if 0 <= cell < 20:
                    column, value = cell, 1.0
                elif 20 <= cell < 40:
                    column, value = 39 - cell, sign(odd, 1)
                else:
                    continue
                for layer in range(2):
                    table[0, layer, row, odd, patch, layer, column] = value
                    table[1, layer, row, odd, patch, 1 - layer, column] = value
    return table.reshape(2, PAIRS, 320).astype(ml_dtypes.bfloat16)


def periodic_basis(length, cells):
    slots = np.arange(length)
    freq = np.where(slots <= length // 2, slots, slots - length // 2)
    weight = np.where((freq == 0) | (freq == length // 2), 1.0, 2.0)
    angle = 2.0 * math.pi / length * (freq[:, None] * cells[None, :] % length)
    basis = np.where((slots <= length // 2)[:, None], np.cos(angle), np.sin(angle))
    return basis * np.sqrt(weight / length)[:, None], freq


REACH = CQ + 2
SIDE = 34
LANES = 384


def far_tables(total_z, total_x, total_y, parts_x, parts_y):
    basis_y, freq_y = periodic_basis(total_y, np.arange(total_y))
    basis_x, freq_x = periodic_basis(total_x, np.arange(total_x))
    along_y = np.zeros((parts_y, 4, 32, 4, total_y))
    for layer in range(4):
        along_y[:, layer, :, layer, :] = basis_y.T.reshape(parts_y, 32, total_y)
    along_y = np.stack(halves(along_y.reshape(parts_y, 128, 4 * total_y)), axis=1)
    high, low = halves(basis_x.reshape(total_x, parts_x, 32).transpose(1, 0, 2))
    along_x = np.concatenate([high, high, low], axis=2)

    def eigen(freq, length):
        return 2.0 - 2.0 * np.cos(2.0 * math.pi / length * freq)

    freq_z = np.arange(total_z)
    square = (
        eigen(freq_z, total_z)[:, None, None]
        + eigen(freq_x, total_x)[None, :, None]
        + eigen(freq_y, total_y)[None, None, :]
    )
    square[0, 0, 0] = 1.0
    inverse = 1.0 / (RATIO * square)
    inverse[0, 0, 0] = 0.0
    steps = np.arange(total_z // 2 + 1)
    cosine = np.cos(2.0 * math.pi / total_z * np.outer(steps, freq_z)) / total_z
    column = np.einsum("dk,kxy->dxy", cosine, inverse).astype(np.float32)

    def windows(length, parts, basis):
        table = np.zeros((parts, 40, length))
        for part in range(parts):
            cells = (np.arange(SIDE) - 1 + part * 32) % length
            table[part, :SIDE] = basis[:, cells].T
        return table.reshape(parts * 40, length)

    square = eigen(freq_x, total_x)[:, None] + eigen(freq_y, total_y)[None, :]
    square[0, 0] = 1.0
    inverse = 1.0 / (RATIO * square)
    inverse[0, 0] = 0.0
    weight = np.outer(basis_x[:, :32].sum(axis=1), basis_y[:, :32].sum(axis=1)) * inverse
    flat = basis_x.T @ weight @ basis_y
    even = np.zeros((parts_x, parts_y, 40, LANES))
    for part in range(parts_x):
        cells_x = (np.arange(SIDE) - 1 + part * 32) % total_x
        for other in range(parts_y):
            cells_y = (np.arange(SIDE) - 1 + other * 32) % total_y
            values = flat[cells_x][:, cells_y].T
            even[part, other, :SIDE, : REACH * SIDE] = np.tile(values, (1, REACH))
    even = even.reshape(parts_x * parts_y, 40, LANES).astype(np.float32)

    back_x = np.concatenate(halves(windows(total_x, parts_x, basis_x)), axis=1)
    back_y = np.stack(halves(windows(total_y, parts_y, basis_y)))
    spread = refine_table(PLACES[:136], np.arange(SIDE) - 1)
    spread_x = np.zeros((REACH, 136, LANES))
    for layer in range(REACH):
        spread_x[layer, :, layer * SIDE : layer * SIDE + SIDE] = spread
    spread_y = np.zeros((40, 256))
    spread_y[:SIDE, :136] = spread.T
    spread_x = spread_x.reshape(REACH * 136, LANES).astype(ml_dtypes.bfloat16)
    spread_y = spread_y.astype(ml_dtypes.bfloat16)
    return along_y, along_x, column, back_x, back_y, even, spread_x, spread_y


def parts_of(values):
    high = values.astype(b16)
    return high, (values - high.astype(f32)).astype(b16)


def mul(left, right):
    return jnp.dot(left, right, preferred_element_type=f32)


def mul_nt(left, right):
    return lax.dot_general(left, right, (((1,), (1,)), ((), ())), preferred_element_type=f32)


def masses_kernel(rho_ref, sum_x_ref, sum_y_ref, out_ref):
    for half in range(2):
        total = jnp.zeros((32, 128), f32)
        for layer in range(4):
            z = (half * 4 + layer) * RATIO
            slab = rho_ref[pl.ds(z, RATIO)].reshape(RATIO * 128, 128)
            rows = mul(sum_x_ref[...], slab)
            high, rest = parts_of(rows)
            mid, low = parts_of(rows - high.astype(f32))
            weights = sum_y_ref[layer]
            total += mul(high, weights) + (mul(mid, weights) + mul(low, weights))
        for copy in range(out_ref.shape[0]):
            out_ref[copy, half * 32 : half * 32 + 32, :] = total


def near_kernel(
    weights_ref,
    rho_ref,
    forward_ref,
    mirror_ref,
    gather_ref,
    coarse_ref,
    backward_ref,
    dense_ref,
    wide_ref,
    upper_ref,
    lower_ref,
    lines,
    smooth,
    spectra,
    turned,
):
    step = pl.program_id(0)

    @pl.when(step == 0)
    def _():
        for z in range(PATCH):
            turned[z] = mul(mirror_ref[...], rho_ref[z]).astype(b16)
        for patch in range(4):
            def rows(mirror_z, mirror_x):
                tiles = []
                for z in range(16):
                    layer = PATCH - 1 - z if mirror_z else z
                    if mirror_x:
                        tiles.append(turned[layer, patch * 16 : patch * 16 + 16, :])
                    else:
                        tiles.append(rho_ref[layer, patch * 32 : patch * 32 + 16, :])
                return jnp.concatenate(tiles, axis=0)

            right = jnp.concatenate([rows(0, 0), rows(0, 1), rows(1, 0), rows(1, 1)], axis=1)

            def chunk(index, carry):
                both = mul_nt(forward_ref[index], right)
                both = both[:128] + both[128:]
                lines[pl.ds(index * 4, 4), :, patch] = both.reshape(4, 4, 8, 256)
                return carry

            lax.fori_loop(0, 12, chunk, 0)
        for parity in range(4):
            values = lines[NF : NF + NC, parity].reshape(NC * 32, 256)
            high, low = parts_of(values)
            sums = mul(high, gather_ref[...]) + mul(low, gather_ref[...])
            high, low = parts_of(sums)
            for freq in range(NC):
                first = high[freq * 32 : freq * 32 + 32]
                second = low[freq * 32 : freq * 32 + 32]
                smooth[freq, parity] = mul(first, coarse_ref[freq, parity, 0]) + (
                    mul(second, coarse_ref[freq, parity, 0])
                    + mul(first, coarse_ref[freq, parity, 1])
                )
        spectra[:, :, 8 * NF :, :] = jnp.zeros((4, 4, 8, 400), f32)

    rest = lax.rem(step, CH)
    alias = jnp.minimum(rest, CH - rest)
    row = lax.broadcasted_iota(jnp.int32, (32, 1), 0)
    weight = jnp.where(row % 8 < 4, weights_ref[step, 0], weights_ref[step, 1])
    for parity in range(4):
        high, low = parts_of(lines[step, parity].reshape(32, 256))
        both = mul_nt(jnp.concatenate([high, low], axis=0), dense_ref[0, parity, 0])
        value = both[:32] + (both[32:] + mul_nt(high, dense_ref[0, parity, 1]))
        value = value - weight * smooth[alias, parity]
        spectra[parity, :, pl.ds(step * 8, 8), :] = value.reshape(4, 8, 400)

    @pl.when(step == NF - 1)
    def _():
        def back(index, carry):
            parity, patch = index // 4, index % 4
            high, low = parts_of(spectra[parity, patch])
            value = mul(backward_ref[0], high) + (
                mul(backward_ref[1], high) + mul(backward_ref[0], low)
            )
            wide_ref[parity, patch] = value[:136]
            upper_ref[parity, patch] = value[136:144]
            lower_ref[parity, patch] = value[144:152]
            return carry

        lax.fori_loop(0, 16, back, 0)


def with_neighbours(values, from_lower, from_upper):
    first = lax.broadcasted_iota(jnp.int32, from_lower.shape, 0) < 4
    zero = jnp.zeros_like(from_lower)
    return jnp.concatenate(
        [
            values[0:8] + jnp.where(first, from_lower, zero),
            values[8:120],
            values[120:128] + jnp.where(first, zero, from_upper),
            values[128:136] + jnp.where(first, from_upper, from_lower),
        ],
        axis=0,
    )


def faces_kernel(wide_ref, from_lower_ref, from_upper_ref, bottom_ref, top_ref):
    even = with_neighbours(wide_ref[0, 0], from_lower_ref[0, 0], from_upper_ref[0, 0])
    odd = with_neighbours(wide_ref[1, 0], from_lower_ref[1, 0], from_upper_ref[1, 0])
    bottom_ref[0] = even + odd
    top_ref[0] = even - odd


def unfold_kernel(
    wide_ref,
    from_lower_ref,
    from_upper_ref,
    from_below_ref,
    from_above_ref,
    unfold_ref,
    near_ref,
    upper_ref,
    lower_ref,
    standing,
    given,
):
    def turn(index, carry):
        even = with_neighbours(wide_ref[0, index], from_lower_ref[0, index], from_upper_ref[0, index])
        odd = with_neighbours(wide_ref[1, index], from_lower_ref[1, index], from_upper_ref[1, index])
        for side, value in ((0, even + odd), (1, even - odd)):
            standing[side, index, :, 0:128] = value[:128].T
            standing[side, index, :, 128:136] = value[128:136].T
        for side, ref in ((0, from_below_ref), (1, from_above_ref)):
            value = ref[index]
            given[side, index, :, 0:128] = value[:128].T
            given[side, index, :, 128:136] = value[128:136].T
        return carry

    lax.fori_loop(0, 8, turn, 0)

    for pair in range(1, 10):
        for side in range(2):
            rows = jnp.concatenate(
                [standing[side, index, 40 * pair : 40 * pair + 40, :] for index in range(8)], axis=0
            )
            high, low = parts_of(rows)
            value = mul(unfold_ref[0], high) + mul(unfold_ref[0], low)
            if pair <= 3:
                other = 3 - pair
                rows = jnp.concatenate(
                    [given[side, index, 40 * other : 40 * other + 40, :] for index in range(8)],
                    axis=0,
                )
                high, low = parts_of(rows)
                value = value + (mul(unfold_ref[1], high) + mul(unfold_ref[1], low))
            for layer in range(2):
                z = 2 * pair + layer
                z = z - 2 if side == 0 else 37 - z
                near_ref[z] = value[160 * layer : 160 * layer + 136]
                upper_ref[z] = value[160 * layer + 136 : 160 * layer + 144]
                lower_ref[z] = value[160 * layer + 144 : 160 * layer + 152]


def far_kernel(
    where_ref,
    masses_ref,
    along_y_ref,
    along_x_ref,
    column_ref,
    back_x_ref,
    back_y_ref,
    even_ref,
    out_ref,
    spectra,
    lines,
    turned,
):
    blocks = masses_ref.shape[0]
    total = spectra.shape[0]
    masses = masses_ref[...].reshape(blocks * 64, 128)
    mean = jnp.sum(masses, axis=(0, 1), keepdims=True) * (1.0 / masses.size)
    high, low = parts_of(masses - mean)
    value = mul(high, along_y_ref[0, 0]) + (
        mul(low, along_y_ref[0, 0]) + mul(high, along_y_ref[0, 1])
    )
    high, low = parts_of(value)
    for half in range(2 * blocks):
        rows = slice(half * 32, half * 32 + 32)
        right = jnp.concatenate([high[rows], low[rows], high[rows]], axis=0)
        value = mul(along_x_ref[0], right)
        for layer in range(4):
            spectra[half * 4 + layer] = value[:, layer * 128 : layer * 128 + 128]

    start = where_ref[2] * CQ

    def solve(tile, carry):
        rows = pl.ds(pl.multiple_of(tile * 8, 8), 8)
        sums = [jnp.zeros((8, 128), f32) for _ in range(REACH)]
        for step in range(total):
            value = spectra[lax.rem(start + step, total), rows, :]
            for layer in range(REACH):
                apart = abs(step - (layer - 1)) % total
                sums[layer] += value * column_ref[min(apart, total - apart), rows, :]
        for layer in range(REACH):
            lines[layer, rows, :] = sums[layer]
        return carry

    lax.fori_loop(0, 16, solve, 0)

    turned[:, REACH * SIDE :, :] = jnp.zeros((4, LANES - REACH * SIDE, 128), f32)
    for layer in range(REACH):
        high, low = parts_of(lines[layer])
        value = mul(back_x_ref[:, 0:128], high) + (
            mul(back_x_ref[:, 0:128], low) + mul(back_x_ref[:, 128:256], high)
        )
        for part in range(4):
            turned[part, layer * SIDE : layer * SIDE + SIDE, :] = value[part * 40 : part * 40 + SIDE]
    for part in range(4):
        high, low = parts_of(turned[part])
        value = mul_nt(back_y_ref[0], high) + (
            mul_nt(back_y_ref[0], low) + mul_nt(back_y_ref[1], high)
        )
        for other in range(4):
            apart = lax.rem(part + 4 - where_ref[0], 4) * 4 + lax.rem(other + 4 - where_ref[1], 4)
            out_ref[part * 4 + other] = value[other * 40 : other * 40 + 40] + mean * even_ref[apart]


def final_kernel(
    near_ref,
    from_lower_ref,
    from_upper_ref,
    far_ref,
    spread_x_ref,
    spread_y_ref,
    potential_ref,
    force_ref,
    whole,
    planes,
    depth,
):
    step = pl.program_id(0)

    @pl.when(step == 0)
    def _():
        sums = far_ref[0]
        for source in range(1, far_ref.shape[0]):
            sums = sums + far_ref[source]
        high, low = parts_of(sums)
        for layer in range(REACH):
            left = spread_x_ref[layer * 136 : layer * 136 + 136, :]
            first, second = parts_of(mul_nt(left, high) + mul_nt(left, low))
            planes[layer] = mul(first, spread_y_ref[...]) + mul(second, spread_y_ref[...])
        for z in range(36):
            place = (z - 2 + 0.5) / RATIO - 0.5
            below = math.floor(place)
            upper = place - below
            value = with_neighbours(near_ref[z], from_lower_ref[z], from_upper_ref[z])
            whole[z] = value + (
                (1.0 - upper) * planes[below + 1] + upper * planes[below + 2]
            )

    row = lax.broadcasted_iota(jnp.int32, (128, 128), 0)
    lane = lax.broadcasted_iota(jnp.int32, (128, 128), 1)

    def difference(plus_one, minus_one, plus_two, minus_two):
        value = -(2.0 / 3.0 * (plus_one - minus_one) - 1.0 / 12.0 * (plus_two - minus_two))
        return value.astype(b16)

    def beyond(values, edge, mask, shift, axis):
        return pltpu.roll(jnp.where(mask, edge, values), shift, axis)

    for inner in range(depth):
        z = step * depth + inner + 2
        here = whole[z, 0:128, 0:128]
        potential_ref[inner] = here
        force_ref[0, inner] = difference(
            whole[z + 1, 0:128, 0:128],
            whole[z - 1, 0:128, 0:128],
            whole[z + 2, 0:128, 0:128],
            whole[z - 2, 0:128, 0:128],
        )
        edge = whole[z, 128:136, 0:128]
        above = jnp.concatenate([edge, here[8:]], axis=0)
        below = jnp.concatenate([here[:120], edge], axis=0)
        force_ref[1, inner] = difference(
            beyond(here, above, row < 1, 127, 0),
            beyond(here, below, row >= 127, 1, 0),
            beyond(here, above, row < 2, 126, 0),
            beyond(here, below, row >= 126, 2, 0),
        )
        above = whole[z, 0:128, 128:256]
        below = pltpu.roll(above, 120, 1)
        force_ref[2, inner] = difference(
            beyond(here, above, lane < 1, 127, 1),
            beyond(here, below, lane >= 127, 1, 1),
            beyond(here, above, lane < 2, 126, 1),
            beyond(here, below, lane >= 126, 2, 1),
        )


VMEM = pl.BlockSpec(memory_space=pltpu.VMEM)
SMEM = pl.BlockSpec(memory_space=pltpu.SMEM)


def params(size):
    return pltpu.CompilerParams(vmem_limit_bytes=size * MIB)


def cost(flops, moved):
    return pl.CostEstimate(flops=int(flops), bytes_accessed=int(moved), transcendentals=0)


def shape(*dims, dtype=f32):
    return jax.ShapeDtypeStruct(dims, dtype)


def make_tables(size_z, size_x, size_y):
    sum_x = np.zeros((32, RATIO, 128))
    for x in range(128):
        sum_x[x // RATIO, :, x] = 1.0
    sum_y = np.zeros((4, 128, 128))
    for layer in range(4):
        for y in range(128):
            sum_y[layer, y, layer * 32 + y // RATIO] = 1.0
    return dict(
        sum_x=sum_x.reshape(32, 512).astype(ml_dtypes.bfloat16),
        sum_y=sum_y.astype(ml_dtypes.bfloat16),
        weights=alias_weights().astype(np.float32),
        forward=forward_table(),
        mirror=mirror_table(),
        gather=gather_table(),
        coarse=coarse_dense_table(),
        backward=backward_table(),
        dense=dense_table(),
        unfold=unfold_table(),
        far=far_tables(size_z * CQ, size_x * 32, size_y * 32, size_x, size_y),
    )


def masses_of(density, tables, copies):
    return pl.pallas_call(
        masses_kernel,
        out_shape=shape(copies, 64, 128),
        in_specs=[VMEM] * 3,
        out_specs=VMEM,
        compiler_params=params(16),
        cost_estimate=cost(2e7, 1.2e6),
        name="masses",
    )(density, tables["sum_x"], tables["sum_y"])


def near_of(density, tables):
    return pl.pallas_call(
        near_kernel,
        grid=(NF,),
        out_shape=(shape(4, 4, 136, 400), shape(4, 4, 8, 400), shape(4, 4, 8, 400)),
        in_specs=[SMEM] + [VMEM] * 6
        + [pl.BlockSpec((1, 4, 2, 400, 256), lambda i: (i, 0, 0, 0, 0))],
        out_specs=(VMEM, VMEM, VMEM),
        scratch_shapes=[
            pltpu.VMEM((NG, 4, 4, 8, 256), f32),
            pltpu.VMEM((NC, 4, 32, 400), f32),
            pltpu.VMEM((4, 4, 304, 400), f32),
            pltpu.VMEM((PATCH, 64, 128), b16),
        ],
        compiler_params=params(56),
        cost_estimate=cost(8e9, 7e7),
        name="near",
    )(
        tables["weights"],
        density,
        tables["forward"],
        tables["mirror"],
        tables["gather"],
        tables["coarse"],
        tables["backward"],
        tables["dense"],
    )


def faces_of(wide, from_lower, from_upper):
    strip = pl.BlockSpec((2, 1, 8, 128), lambda i: (0, i, 0, 0))
    face = pl.BlockSpec((1, 136, 128), lambda i: (i, 0, 0))
    return pl.pallas_call(
        faces_kernel,
        grid=(8,),
        out_shape=(shape(8, 136, 128), shape(8, 136, 128)),
        in_specs=[pl.BlockSpec((2, 1, 136, 128), lambda i: (0, i, 0, 0)), strip, strip],
        out_specs=(face, face),
        compiler_params=params(16),
        cost_estimate=cost(1e6, 2.5e6),
        name="faces",
    )(wide, from_lower, from_upper)


def unfold_of(wide, from_lower, from_upper, from_below, from_above, tables):
    return pl.pallas_call(
        unfold_kernel,
        out_shape=(shape(36, 136, 256), shape(36, 8, 256), shape(36, 8, 256)),
        in_specs=[VMEM] * 6,
        out_specs=(VMEM, VMEM, VMEM),
        scratch_shapes=[
            pltpu.VMEM((2, 8, 400, 256), f32),
            pltpu.VMEM((2, 8, 128, 256), f32),
        ],
        compiler_params=params(56),
        cost_estimate=cost(4e9, 1.2e7),
        name="unfold",
    )(wide, from_lower, from_upper, from_below, from_above, tables["unfold"])


def far_of(where, masses, tables):
    along_y, along_x, column, back_x, back_y, even = tables["far"][:6]
    parts = along_x.shape[0] * along_y.shape[0]
    total = masses.shape[0] * CQ

    def fixed(*dims):
        return pl.BlockSpec(dims, lambda i, w: (0,) * len(dims))

    return pl.pallas_call(
        far_kernel,
        grid_spec=pltpu.PrefetchScalarGridSpec(
            num_scalar_prefetch=1,
            grid=(1,),
            in_specs=[
                fixed(*masses.shape),
                pl.BlockSpec((1, 2, 128, 512), lambda i, w: (w[1], 0, 0, 0)),
                pl.BlockSpec((1, 128, 96), lambda i, w: (w[0], 0, 0)),
                fixed(*column.shape),
                fixed(*back_x.shape),
                fixed(*back_y.shape),
                fixed(*even.shape),
            ],
            out_specs=fixed(parts, 40, LANES),
            scratch_shapes=[
                pltpu.VMEM((total, 128, 128), f32),
                pltpu.VMEM((REACH, 128, 128), f32),
                pltpu.VMEM((4, LANES, 128), f32),
            ],
        ),
        out_shape=shape(parts, 40, LANES),
        compiler_params=params(48),
        cost_estimate=cost(4e9, 9e6),
        name="far",
    )(where, masses, along_y, along_x, column, back_x, back_y, even)


def final_of(near, from_lower, from_upper, far, tables):
    depth = 4
    strip = pl.BlockSpec((36, 8, 256), lambda i: (0, 0, 0))
    return pl.pallas_call(
        functools.partial(final_kernel, depth=depth),
        grid=(PATCH // depth,),
        out_shape=(shape(PATCH, 128, 128), shape(3, PATCH, 128, 128, dtype=b16)),
        in_specs=[
            pl.BlockSpec((36, 136, 256), lambda i: (0, 0, 0)),
            strip,
            strip,
            pl.BlockSpec(far.shape, lambda i: (0, 0, 0)),
            pl.BlockSpec((REACH * 136, LANES), lambda i: (0, 0)),
            pl.BlockSpec((40, 256), lambda i: (0, 0)),
        ],
        out_specs=(
            pl.BlockSpec((depth, 128, 128), lambda i: (i, 0, 0)),
            pl.BlockSpec((3, depth, 128, 128), lambda i: (0, i, 0, 0)),
        ),
        scratch_shapes=[pltpu.VMEM((36, 136, 256), f32), pltpu.VMEM((REACH, 136, 256), f32)],
        compiler_params=params(48),
        cost_estimate=cost(2e8, 1.2e7),
        name="final",
    )(near, from_lower, from_upper, far, *tables["far"][6:])


def exchange(upper, lower, axis):
    count = lax.axis_size(axis)
    up = [(i, (i + 1) % count) for i in range(count)]
    down = [(target, source) for source, target in up]
    return lax.ppermute(upper, axis, up), lax.ppermute(lower, axis, down)


def body(tables, density):
    size_gz = lax.axis_size("gz")
    where = jnp.stack([lax.axis_index(axis) for axis in ("gx", "gy", "gz")]).astype(jnp.int32)
    masses = masses_of(density, tables, size_gz)
    masses = lax.all_to_all(masses, "gz", 0, 0, tiled=True)
    wide, upper, lower = near_of(density, tables)
    wide = wide.reshape(2, 8, 136, 400)
    from_lower, from_upper = exchange(upper, lower, "gy")
    from_lower = from_lower.reshape(2, 8, 8, 400)
    from_upper = from_upper.reshape(2, 8, 8, 400)
    far = far_of(where, masses, tables)
    far = lax.all_to_all(far, ("gx", "gy"), 0, 0, tiled=True)
    bottom, top = faces_of(wide, from_lower, from_upper)
    from_below, from_above = exchange(top, bottom, "gz")
    near, upper, lower = unfold_of(wide, from_lower, from_upper, from_below, from_above, tables)
    from_lower, from_upper = exchange(upper, lower, "gx")
    return final_of(near, from_lower, from_upper, far, tables)


def solution(mesh):
    tables = make_tables(mesh.shape["gz"], mesh.shape["gx"], mesh.shape["gy"])
    return jax.shard_map(
        functools.partial(body, tables),
        mesh=mesh,
        in_specs=(P("gz", "gx", "gy"),),
        out_specs=(P("gz", "gx", "gy"), P(None, "gz", "gx", "gy")),
        check_vma=False,
    )
```

```python
import functools
import math

import jax
import jax.numpy as jnp
import ml_dtypes
import numpy as np
from jax import lax
from jax.experimental import pallas as pl
from jax.experimental.pallas import tpu as pltpu
from jax.sharding import PartitionSpec as P

HOCK = 72
RATIO = 4
PATCH = 32
CQ = 8
CH = HOCK // RATIO
NF = HOCK // 2 + 1
NC = CH // 2 + 1
NG = 48
NR = 40
RING = 16
ROWS = 1056
PAIRS = 320

f32 = jnp.float32
b16 = jnp.bfloat16
MIB = 1 << 20


def halves(table):
    high = table.astype(ml_dtypes.bfloat16)
    low = (table - high.astype(np.float64)).astype(ml_dtypes.bfloat16)
    return high, low


def centred(length, cells, centre):
    freq = np.arange(length // 2 + 1)
    weight = np.where((freq == 0) | (freq == length // 2), 1.0, 2.0)
    angle = 2.0 * math.pi / length * freq[:, None] * (cells - centre)[None, :]
    basis = np.stack([np.cos(angle), np.sin(angle)], axis=1)
    basis *= np.sqrt(weight / length)[:, None, None]
    return np.where(np.abs(basis) < 1e-12, 0.0, basis)


def fine_basis(cells):
    return centred(HOCK, cells, (PATCH - 1) / 2)


def coarse_basis(cells):
    return centred(CH, cells, (CQ - 1) / 2)


def inverse_distance(square, ratio):
    return np.where(
        square > 0, 1.0 / (4.0 * math.pi * ratio * np.sqrt(np.maximum(square, 1))), 0.25 / ratio
    )


def line_spectra(length, reach, ratio):
    index = np.arange(length)
    wrap = np.minimum(index, length - index)
    side = np.arange(reach)
    square = side[:, None, None] ** 2 + side[None, :, None] ** 2 + wrap[None, None, :] ** 2
    kernel = inverse_distance(square, ratio)
    cosine = np.cos(2.0 * math.pi / length * np.outer(np.arange(length // 2 + 1), index))
    return np.einsum("fd,abd->fab", cosine, kernel)


def refine_table(fine, coarse):
    return np.maximum(0.0, 1.0 - np.abs((fine[:, None] + 0.5) / RATIO - 0.5 - coarse[None, :]))


def sign(odd, mirrored):
    return -1.0 if (odd and mirrored) else 1.0


def swap_pairs(count):
    first, second = np.triu_indices(count)
    above, beyond = np.triu_indices(count, 1)
    return (first, second), (above, beyond)


def dense_table():
    spectra = line_spectra(HOCK, 36, 1)
    target = np.arange(20)[None, :] - RATIO
    source = np.arange(16)[:, None]
    near, far = np.abs(target - source), np.abs(target - (PATCH - 1 - source))

    def pick(first, second):
        return spectra[:, first[:, None, :, None], second[None, :, None, :]]

    terms = {(a, b): pick((near, far)[a], (near, far)[b]) for a in (0, 1) for b in (0, 1)}
    table = np.zeros((NF, ROWS, 256))
    for parity in range(4):
        odd_z, odd_x = divmod(parity, 2)
        if parity == 2:
            continue
        total = sum(sign(odd_z, a) * sign(odd_x, b) * terms[a, b] for a in (0, 1) for b in (0, 1))
        total = 0.25 * total
        if parity == 1:
            flat = total.reshape(NF, 256, 400)
            table[:, 544:800] = flat[:, :, :256]
            table[:, 800:1056, :144] = flat[:, :, 256:]
            continue
        base = 0 if parity == 0 else 272
        whole_in, strict_in = swap_pairs(16)
        whole_out, strict_out = swap_pairs(20)
        swapped = total.transpose(0, 2, 1, 3, 4)
        both, less = 0.5 * (total + swapped), 0.5 * (total - swapped)
        table[:, base : base + 136, :210] = both[:, whole_in[0], whole_in[1]][
            :, :, whole_out[0], whole_out[1]
        ]
        table[:, base + 144 : base + 264, :190] = less[:, strict_in[0], strict_in[1]][
            :, :, strict_out[0], strict_out[1]
        ]
    result = np.empty((NF, 2, ROWS, 256), ml_dtypes.bfloat16)
    result[:, 0], result[:, 1] = halves(table)
    return result


def swap_tables():
    whole, strict = swap_pairs(16)
    inward = np.zeros((16, 16, 384))
    spots = np.arange(136)
    inward[whole[0], whole[1], spots] = 1.0
    inward[whole[1], whole[0], spots] = 1.0
    spots = 256 + np.arange(120)
    inward[strict[0], strict[1], spots] = 1.0
    inward[strict[1], strict[0], spots] = -1.0
    whole, strict = swap_pairs(20)
    outward = np.zeros((2, 512, 20, 20))
    spots = np.arange(210)
    outward[0, spots, whole[0], whole[1]] = 1.0
    outward[0, spots, whole[1], whole[0]] = 1.0
    spots = 256 + np.arange(190)
    outward[0, spots, strict[0], strict[1]] = 1.0
    outward[0, spots, strict[1], strict[0]] = -1.0
    outward[1, :400] = np.eye(400).reshape(20, 20, 20, 20).transpose(1, 0, 2, 3).reshape(400, 20, 20)
    turn = np.eye(256).reshape(16, 16, 16, 16).transpose(1, 0, 2, 3).reshape(256, 256)
    return tuple(
        table.astype(ml_dtypes.bfloat16)
        for table in (inward.reshape(256, 384), turn, outward.reshape(2, 512, 400))
    )


def coarse_dense_table():
    spectra = line_spectra(CH, 10, RATIO)
    window = np.arange(-2, CQ + 2)
    apart = np.abs(window[:, None] - np.arange(CQ)[None, :])
    kernel = spectra[:, apart[:, None, :, None], apart[None, :, None, :]]
    spread = refine_table(np.arange(20) - RATIO, window)
    kernel = np.einsum("za,xb,fabcd->fcdzx", spread, spread, kernel)
    whole, strict = swap_pairs(20)
    result = np.empty((NC, 4, 2, 16, 512), ml_dtypes.bfloat16)
    for parity in range(4):
        odd_z, odd_x = divmod(parity, 2)
        mirrored = kernel[:, ::-1]
        total = kernel + (-1.0) ** odd_z * mirrored
        total = total + (-1.0) ** odd_x * total[:, :, ::-1]
        total = 0.25 * total[:, :4, :4].reshape(NC, 16, 20, 20)
        swapped = total.transpose(0, 1, 3, 2)
        table = np.zeros((NC, 16, 512))
        if parity == 1:
            table[:, :, :400] = total.reshape(NC, 16, 400)
        elif parity == 2:
            table[:, :, :400] = swapped.reshape(NC, 16, 400)
        else:
            table[:, :, :210] = (0.5 * (total + swapped))[:, :, whole[0], whole[1]]
            table[:, :, 256:446] = (0.5 * (total - swapped))[:, :, strict[0], strict[1]]
        result[:, parity, 0], result[:, parity, 1] = halves(table)
    return result


def forward_table():
    cells = np.arange(PATCH)
    lines = np.zeros((NG, 2, PATCH))
    lines[:NF] = fine_basis(cells)
    lines[NF : NF + NC] = coarse_basis(cells // RATIO)
    table = np.zeros((NG, 2, 4, 4, PATCH))
    for patch in range(4):
        table[:, :, patch, patch] = lines
    high, low = halves(table.reshape(4, 96, 128))
    return np.concatenate([high, low], axis=1)


def mirror_table():
    table = np.zeros((64, 128))
    for patch in range(4):
        for cell in range(16):
            table[patch * 16 + cell, patch * 32 + 31 - cell] = 1.0
    return table.astype(ml_dtypes.bfloat16)


def gather_table():
    table = np.zeros((16, 16, 4, 4))
    for z in range(16):
        for x in range(16):
            table[z, x, z // RATIO, x // RATIO] = 1.0
    return table.reshape(256, 16).astype(ml_dtypes.bfloat16)


def alias_weights():
    fine = np.arange(HOCK)
    spread = np.zeros((HOCK, CH))
    for shift in (-1, 0, 1):
        spread += refine_table(fine, np.arange(CH) + shift * CH)
    mapped = np.einsum("fct,tY,GcY->fcG", fine_basis(fine), spread, coarse_basis(np.arange(CH)))
    rest = np.arange(NF) % CH
    alias = np.minimum(rest, CH - rest)
    return mapped[np.arange(NF), :, alias]


BLOCK = 128
BEYOND = [128, 129, 130, 131, -4, -3, -2, -1]
UPPER = [128, 129, 130, 131, 124, 125, 126, 127]
LOWER = [0, 1, 2, 3, -4, -3, -2, -1]
PLACES = np.array(list(range(BLOCK)) + BEYOND + UPPER + LOWER)


def backward_table():
    table = np.zeros((160, 38, 2, 4))
    for patch in range(4):
        cells = PLACES - PATCH * patch
        inside = (cells >= -RATIO) & (cells < PATCH + RATIO)
        values = fine_basis(cells) * inside
        table[:152, :NF, :, patch] = values.transpose(2, 0, 1)
    return np.stack(halves(table.reshape(160, 304)))


def unfold_table():
    table = np.zeros((2, 2, 160, 2, 4, 2, 20))
    for odd in range(2):
        for patch in range(4):
            for row, place in enumerate(PLACES):
                cell = place - PATCH * patch + RATIO
                if 0 <= cell < 20:
                    column, value = cell, 1.0
                elif 20 <= cell < 40:
                    column, value = 39 - cell, sign(odd, 1)
                else:
                    continue
                for layer in range(2):
                    table[0, layer, row, odd, patch, layer, column] = value
                    table[1, layer, row, odd, patch, 1 - layer, column] = value
    return table.reshape(2, PAIRS, 320).astype(ml_dtypes.bfloat16)


def periodic_basis(length, cells):
    slots = np.arange(length)
    freq = np.where(slots <= length // 2, slots, slots - length // 2)
    weight = np.where((freq == 0) | (freq == length // 2), 1.0, 2.0)
    angle = 2.0 * math.pi / length * (freq[:, None] * cells[None, :] % length)
    basis = np.where((slots <= length // 2)[:, None], np.cos(angle), np.sin(angle))
    return basis * np.sqrt(weight / length)[:, None], freq


REACH = CQ + 2
SIDE = 34
LANES = 384


def far_tables(total_z, total_x, total_y, parts_x, parts_y):
    basis_y, freq_y = periodic_basis(total_y, np.arange(total_y))
    basis_x, freq_x = periodic_basis(total_x, np.arange(total_x))
    along_y = np.zeros((parts_y, 4, 32, 4, total_y))
    for layer in range(4):
        along_y[:, layer, :, layer, :] = basis_y.T.reshape(parts_y, 32, total_y)
    along_y = np.stack(halves(along_y.reshape(parts_y, 128, 4 * total_y)), axis=1)
    high, low = halves(basis_x.reshape(total_x, parts_x, 32).transpose(1, 0, 2))
    along_x = np.concatenate([high, high, low], axis=2)

    def eigen(freq, length):
        return 2.0 - 2.0 * np.cos(2.0 * math.pi / length * freq)

    freq_z = np.arange(total_z)
    square = (
        eigen(freq_z, total_z)[:, None, None]
        + eigen(freq_x, total_x)[None, :, None]
        + eigen(freq_y, total_y)[None, None, :]
    )
    square[0, 0, 0] = 1.0
    inverse = 1.0 / (RATIO * square)
    inverse[0, 0, 0] = 0.0
    steps = np.arange(total_z // 2 + 1)
    cosine = np.cos(2.0 * math.pi / total_z * np.outer(steps, freq_z)) / total_z
    column = np.einsum("dk,kxy->dxy", cosine, inverse).astype(np.float32)

    def windows(length, parts, basis):
        table = np.zeros((parts, 40, length))
        for part in range(parts):
            cells = (np.arange(SIDE) - 1 + part * 32) % length
            table[part, :SIDE] = basis[:, cells].T
        return table.reshape(parts * 40, length)

    square = eigen(freq_x, total_x)[:, None] + eigen(freq_y, total_y)[None, :]
    square[0, 0] = 1.0
    inverse = 1.0 / (RATIO * square)
    inverse[0, 0] = 0.0
    weight = np.outer(basis_x[:, :32].sum(axis=1), basis_y[:, :32].sum(axis=1)) * inverse
    flat = basis_x.T @ weight @ basis_y
    even = np.zeros((parts_x, parts_y, 40, LANES))
    for part in range(parts_x):
        cells_x = (np.arange(SIDE) - 1 + part * 32) % total_x
        for other in range(parts_y):
            cells_y = (np.arange(SIDE) - 1 + other * 32) % total_y
            values = flat[cells_x][:, cells_y].T
            even[part, other, :SIDE, : REACH * SIDE] = np.tile(values, (1, REACH))
    even = even.reshape(parts_x * parts_y, 40, LANES).astype(np.float32)

    back_x = np.concatenate(halves(windows(total_x, parts_x, basis_x)), axis=1)
    back_y = np.stack(halves(windows(total_y, parts_y, basis_y)))
    spread = refine_table(PLACES[:136], np.arange(SIDE) - 1)
    spread_x = np.zeros((REACH, 136, LANES))
    for layer in range(REACH):
        spread_x[layer, :, layer * SIDE : layer * SIDE + SIDE] = spread
    spread_y = np.zeros((40, 256))
    spread_y[:SIDE, :136] = spread.T
    spread_x = spread_x.reshape(REACH * 136, LANES).astype(ml_dtypes.bfloat16)
    spread_y = spread_y.astype(ml_dtypes.bfloat16)
    return along_y, along_x, column, back_x, back_y, even, spread_x, spread_y


def parts_of(values):
    high = values.astype(b16)
    return high, (values - high.astype(f32)).astype(b16)


def mul(left, right):
    return jnp.dot(left, right, preferred_element_type=f32)


def mul_nt(left, right):
    return lax.dot_general(left, right, (((1,), (1,)), ((), ())), preferred_element_type=f32)


def masses_kernel(rho_ref, out_ref):
    row = lax.broadcasted_iota(jnp.int32, (32, 512), 0)
    column = lax.broadcasted_iota(jnp.int32, (32, 512), 1)
    sum_x = jnp.where(column % 128 // RATIO == row, 1.0, 0.0).astype(b16)
    row = lax.broadcasted_iota(jnp.int32, (128, 128), 0)
    column = lax.broadcasted_iota(jnp.int32, (128, 128), 1)
    for half in range(2):
        total = jnp.zeros((32, 128), f32)
        for layer in range(4):
            z = (half * 4 + layer) * RATIO
            slab = rho_ref[pl.ds(z, RATIO)].reshape(RATIO * 128, 128)
            rows = mul(sum_x, slab)
            high, rest = parts_of(rows)
            mid, low = parts_of(rows - high.astype(f32))
            weights = jnp.where(row // RATIO + layer * 32 == column, 1.0, 0.0).astype(b16)
            total += mul(high, weights) + (mul(mid, weights) + mul(low, weights))
        for copy in range(out_ref.shape[0]):
            out_ref[copy, half * 32 : half * 32 + 32, :] = total


def mul_pairs(values, high_table, low_table):
    rows = values.shape[0]
    high, low = parts_of(values)
    both = mul(jnp.concatenate([high, low], axis=0), high_table)
    return both[:rows] + (both[rows:] + mul(high, low_table))


def mul_exact(values, table):
    rows = values.shape[0]
    high, low = parts_of(values)
    both = mul(jnp.concatenate([high, low], axis=0), table)
    return both[:rows] + both[rows:]


def near_kernel(
    weights_ref,
    rho_ref,
    forward_ref,
    mirror_ref,
    gather_ref,
    coarse_ref,
    backward_ref,
    inward_ref,
    turn_ref,
    outward_ref,
    dense_ref,
    wide_ref,
    upper_ref,
    lower_ref,
    bottom_ref,
    top_ref,
    lines,
    ready,
    smooth,
    spectra,
    turned,
    ring,
    arrived,
):
    def fetch(freq, slot):
        return pltpu.make_async_copy(dense_ref.at[freq], ring.at[slot], arrived.at[slot])

    for slot in range(RING):
        fetch(slot, slot).start()

    for z in range(PATCH):
        turned[z] = mul(mirror_ref[...], rho_ref[z]).astype(b16)
    for patch in range(4):
        def rows(mirror_z, mirror_x):
            tiles = []
            for z in range(16):
                layer = PATCH - 1 - z if mirror_z else z
                if mirror_x:
                    tiles.append(turned[layer, patch * 16 : patch * 16 + 16, :])
                else:
                    tiles.append(rho_ref[layer, patch * 32 : patch * 32 + 16, :])
            return jnp.concatenate(tiles, axis=0)

        right = [rows(0, 0), rows(0, 1), rows(1, 0), rows(1, 1)]

        def chunk(index, carry):
            left = forward_ref[index]
            sums = []
            for mirror in range(4):
                both = mul_nt(left, right[mirror])
                sums.append(both[:96] + both[96:])
            even, odd = sums[0] + sums[1], sums[0] - sums[1]
            even_far, odd_far = sums[2] + sums[3], sums[2] - sums[3]
            freqs = pl.ds(index * 12, 12)
            lines[freqs, 0, patch] = (even + even_far).reshape(12, 8, 256)
            lines[freqs, 1, patch] = (odd + odd_far).reshape(12, 8, 256)
            lines[freqs, 2, patch] = (even - even_far).reshape(12, 8, 256)
            lines[freqs, 3, patch] = (odd - odd_far).reshape(12, 8, 256)
            return carry

        lax.fori_loop(0, 4, chunk, 0)

    for parity in range(4):
        values = lines[NF : NF + NC, parity].reshape(NC * 32, 256)
        high, low = parts_of(mul_exact(values, gather_ref[...]))
        for freq in range(NC):
            both = jnp.concatenate(
                [high[freq * 32 : freq * 32 + 32], low[freq * 32 : freq * 32 + 32]], axis=0
            )
            value = mul(both, coarse_ref[freq, parity, 0])
            smooth[freq, parity] = value[:32] + (
                value[32:] + mul(both[:32], coarse_ref[freq, parity, 1])
            )

    def prepare(index, carry):
        freqs = pl.ds(index * 4, 4)
        for slot, parity in ((0, 0), (1, 3)):
            values = lines[freqs, parity].reshape(128, 256)
            ready[freqs, slot] = mul_exact(values, inward_ref[...]).reshape(4, 32, 384)
        values = lines[freqs, 2].reshape(128, 256)
        ready[freqs, 2, :, 0:256] = mul_exact(values, turn_ref[...]).reshape(4, 32, 256)
        return carry

    lax.fori_loop(0, NR // 4, prepare, 0)
    spectra[:, :, 8 * NF :, :] = jnp.zeros((4, 4, 8, 512), f32)
    row = lax.broadcasted_iota(jnp.int32, (32, 1), 0)

    def solve(freq, carry):
        slot = lax.rem(freq, RING)
        fetch(freq, slot).wait()
        rest = lax.rem(freq, CH)
        alias = jnp.minimum(rest, CH - rest)
        weight = jnp.where(row % 8 < 4, weights_ref[freq, 0], weights_ref[freq, 1])
        here = pl.ds(freq * 8, 8)

        def keep(parity, low, high, value):
            value = value - weight * smooth[alias, parity, :, low:high]
            spectra[parity, :, here, low:high] = value.reshape(4, 8, 256)

        for place, parity in ((0, 0), (1, 3)):
            for base, count, lane in ((0, 144, 0), (144, 128, 256)):
                base = base + 272 * place
                value = mul_pairs(
                    ready[freq, place, :, lane : lane + count],
                    ring[slot, 0, base : base + count, :],
                    ring[slot, 1, base : base + count, :],
                )
                keep(parity, lane, lane + 256, value)
        values = jnp.concatenate(
            [lines[freq, 1].reshape(32, 256), ready[freq, 2, :, 0:256]], axis=0
        )
        for base, lane in ((544, 0), (800, 256)):
            value = mul_pairs(
                values, ring[slot, 0, base : base + 256, :], ring[slot, 1, base : base + 256, :]
            )
            keep(1, lane, lane + 256, value[:32])
            keep(2, lane, lane + 256, value[32:])

        @pl.when(freq + RING < NF)
        def _():
            fetch(freq + RING, slot).start()

        return carry

    lax.fori_loop(0, NF, solve, 0)

    for parity in range(4):
        def back(patch, carry):
            high, low = parts_of(spectra[parity, patch])
            value = mul(backward_ref[0], high) + (
                mul(backward_ref[1], high) + mul(backward_ref[0], low)
            )
            if parity != 1:
                value = mul_exact(value, outward_ref[1 if parity == 2 else 0])
            wide_ref[parity, patch] = value[:136, :400]
            upper_ref[parity, patch] = value[136:144, :400]
            lower_ref[parity, patch] = value[144:152, :400]
            return carry

        lax.fori_loop(0, 4, back, 0)

    for odd_x in range(2):
        for patch in range(4):
            index = odd_x * 4 + patch
            even = wide_ref[odd_x, patch, :, 0:128]
            odd = wide_ref[2 + odd_x, patch, :, 0:128]
            bottom_ref[index] = even + odd
            top_ref[index] = even - odd


def with_neighbours(values, from_lower, from_upper):
    first = lax.broadcasted_iota(jnp.int32, from_lower.shape, 0) < 4
    zero = jnp.zeros_like(from_lower)
    return jnp.concatenate(
        [
            values[0:8] + jnp.where(first, from_lower, zero),
            values[8:120],
            values[120:128] + jnp.where(first, zero, from_upper),
            values[128:136] + jnp.where(first, from_upper, from_lower),
        ],
        axis=0,
    )


def turned_into(ref, side, index, value):
    ref[side, index, :, 0:128] = value[:128].T
    ref[side, index, :, 128:136] = value[128:136].T


def rows_of(ref, side, pair):
    rows = slice(40 * pair, 40 * pair + 40)
    return jnp.concatenate([ref[side, index, rows, :] for index in range(8)], axis=0)


def unfolded(table, rows):
    high, low = parts_of(rows)
    return mul(table, high) + mul(table, low)


def store_layers(value, places, near_ref, upper_ref, lower_ref):
    for layer, z in enumerate(places):
        near_ref[z] = value[160 * layer : 160 * layer + 136]
        upper_ref[z] = value[160 * layer + 136 : 160 * layer + 144]
        lower_ref[z] = value[160 * layer + 144 : 160 * layer + 152]


def inner_kernel(
    wide_ref,
    from_lower_ref,
    from_upper_ref,
    unfold_ref,
    near_ref,
    upper_ref,
    lower_ref,
    outer_ref,
    standing,
):
    def turn(index, carry):
        even = with_neighbours(wide_ref[0, index], from_lower_ref[0, index], from_upper_ref[0, index])
        odd = with_neighbours(wide_ref[1, index], from_lower_ref[1, index], from_upper_ref[1, index])
        turned_into(standing, 0, index, even + odd)
        turned_into(standing, 1, index, even - odd)
        return carry

    lax.fori_loop(0, 8, turn, 0)
    outer_ref[...] = standing[:, :, 40:160, :]
    for pair in range(4, 10):
        for side in range(2):
            value = unfolded(unfold_ref[0], rows_of(standing, side, pair))
            places = [2 * pair - 8, 2 * pair - 7]
            if side == 1:
                places = [23 - z for z in places]
            store_layers(value, places, near_ref, upper_ref, lower_ref)


def outer_kernel(
    outer_ref,
    from_below_ref,
    from_above_ref,
    corner_lower_ref,
    corner_upper_ref,
    unfold_ref,
    near_ref,
    upper_ref,
    lower_ref,
    given,
):
    def turn(index, carry):
        for side, ref in ((0, from_below_ref), (1, from_above_ref)):
            value = with_neighbours(
                ref[index], corner_lower_ref[side, index], corner_upper_ref[side, index]
            )
            turned_into(given, side, index, value)
        return carry

    lax.fori_loop(0, 8, turn, 0)
    for pair in range(3):
        for side in range(2):
            value = unfolded(unfold_ref[0], rows_of(outer_ref, side, pair))
            value = value + unfolded(unfold_ref[1], rows_of(given, side, 2 - pair))
            places = [2 * pair, 2 * pair + 1]
            if side == 1:
                places = [11 - z for z in places]
            store_layers(value, places, near_ref, upper_ref, lower_ref)


def far_kernel(
    where_ref,
    masses_ref,
    along_y_ref,
    along_x_ref,
    column_ref,
    back_x_ref,
    back_y_ref,
    even_ref,
    out_ref,
    spectra,
    lines,
    turned,
):
    blocks = masses_ref.shape[0]
    total = spectra.shape[0]
    masses = masses_ref[...].reshape(blocks * 64, 128)
    mean = jnp.sum(masses, axis=(0, 1), keepdims=True) * (1.0 / masses.size)
    high, low = parts_of(masses - mean)
    value = mul(high, along_y_ref[0, 0]) + (
        mul(low, along_y_ref[0, 0]) + mul(high, along_y_ref[0, 1])
    )
    high, low = parts_of(value)
    for half in range(2 * blocks):
        rows = slice(half * 32, half * 32 + 32)
        right = jnp.concatenate([high[rows], low[rows], high[rows]], axis=0)
        value = mul(along_x_ref[0], right)
        for layer in range(4):
            spectra[half * 4 + layer] = value[:, layer * 128 : layer * 128 + 128]

    start = where_ref[2] * CQ

    def solve(tile, carry):
        rows = pl.ds(pl.multiple_of(tile * 8, 8), 8)
        sums = [jnp.zeros((8, 128), f32) for _ in range(REACH)]
        for step in range(total):
            value = spectra[lax.rem(start + step, total), rows, :]
            for layer in range(REACH):
                apart = abs(step - (layer - 1)) % total
                sums[layer] += value * column_ref[min(apart, total - apart), rows, :]
        for layer in range(REACH):
            lines[layer, rows, :] = sums[layer]
        return carry

    lax.fori_loop(0, 16, solve, 0)

    turned[:, REACH * SIDE :, :] = jnp.zeros((4, LANES - REACH * SIDE, 128), f32)
    for layer in range(REACH):
        high, low = parts_of(lines[layer])
        value = mul(back_x_ref[:, 0:128], high) + (
            mul(back_x_ref[:, 0:128], low) + mul(back_x_ref[:, 128:256], high)
        )
        for part in range(4):
            turned[part, layer * SIDE : layer * SIDE + SIDE, :] = value[part * 40 : part * 40 + SIDE]
    for part in range(4):
        high, low = parts_of(turned[part])
        value = mul_nt(back_y_ref[0], high) + (
            mul_nt(back_y_ref[0], low) + mul_nt(back_y_ref[1], high)
        )
        for other in range(4):
            apart = lax.rem(part + 4 - where_ref[0], 4) * 4 + lax.rem(other + 4 - where_ref[1], 4)
            out_ref[part * 4 + other] = value[other * 40 : other * 40 + 40] + mean * even_ref[apart]


def planes_kernel(far_ref, spread_x_ref, spread_y_ref, out_ref):
    sums = far_ref[0]
    for source in range(1, far_ref.shape[0]):
        sums = sums + far_ref[source]
    high, low = parts_of(sums)
    for layer in range(REACH):
        left = spread_x_ref[layer * 136 : layer * 136 + 136, :]
        value = mul_nt(left, high) + mul_nt(left, low)
        first, second = parts_of(value)
        out_ref[layer] = mul(first, spread_y_ref[...]) + mul(second, spread_y_ref[...])


def final_kernel(
    inner_ref,
    inner_lower_ref,
    inner_upper_ref,
    outer_ref,
    outer_lower_ref,
    outer_upper_ref,
    planes_ref,
    potential_ref,
    force_ref,
    whole,
    depth,
):
    step = pl.program_id(0)

    @pl.when(step == 0)
    def _():
        for z in range(36):
            place = (z - 2 + 0.5) / RATIO - 0.5
            below = math.floor(place)
            share = place - below
            if 6 <= z < 30:
                refs, spot = (inner_ref, inner_lower_ref, inner_upper_ref), z - 6
            else:
                refs, spot = (outer_ref, outer_lower_ref, outer_upper_ref), z % 24
            value = with_neighbours(*(ref[spot] for ref in refs))
            whole[z] = value + (
                (1.0 - share) * planes_ref[below + 1] + share * planes_ref[below + 2]
            )

    row = lax.broadcasted_iota(jnp.int32, (128, 128), 0)
    lane = lax.broadcasted_iota(jnp.int32, (128, 128), 1)

    def difference(plus_one, minus_one, plus_two, minus_two):
        value = -(2.0 / 3.0 * (plus_one - minus_one) - 1.0 / 12.0 * (plus_two - minus_two))
        return value.astype(b16)

    def beyond(values, edge, mask, shift, axis):
        return pltpu.roll(jnp.where(mask, edge, values), shift, axis)

    for inner in range(depth):
        z = step * depth + inner + 2
        here = whole[z, 0:128, 0:128]
        potential_ref[inner] = here
        force_ref[0, inner] = difference(
            whole[z + 1, 0:128, 0:128],
            whole[z - 1, 0:128, 0:128],
            whole[z + 2, 0:128, 0:128],
            whole[z - 2, 0:128, 0:128],
        )
        edge = whole[z, 128:136, 0:128]
        above = jnp.concatenate([edge, here[8:]], axis=0)
        below = jnp.concatenate([here[:120], edge], axis=0)
        force_ref[1, inner] = difference(
            beyond(here, above, row < 1, 127, 0),
            beyond(here, below, row >= 127, 1, 0),
            beyond(here, above, row < 2, 126, 0),
            beyond(here, below, row >= 126, 2, 0),
        )
        above = whole[z, 0:128, 128:256]
        below = pltpu.roll(above, 120, 1)
        force_ref[2, inner] = difference(
            beyond(here, above, lane < 1, 127, 1),
            beyond(here, below, lane >= 127, 1, 1),
            beyond(here, above, lane < 2, 126, 1),
            beyond(here, below, lane >= 126, 2, 1),
        )


VMEM = pl.BlockSpec(memory_space=pltpu.VMEM)
SMEM = pl.BlockSpec(memory_space=pltpu.SMEM)


def params(size):
    return pltpu.CompilerParams(vmem_limit_bytes=size * MIB)


def cost(flops, moved):
    return pl.CostEstimate(flops=int(flops), bytes_accessed=int(moved), transcendentals=0)


def shape(*dims, dtype=f32):
    return jax.ShapeDtypeStruct(dims, dtype)


def make_tables(size_z, size_x, size_y):
    return dict(
        weights=alias_weights().astype(np.float32),
        forward=forward_table(),
        mirror=mirror_table(),
        gather=gather_table(),
        coarse=coarse_dense_table(),
        backward=backward_table(),
        dense=dense_table(),
        swap=swap_tables(),
        unfold=unfold_table(),
        far=far_tables(size_z * CQ, size_x * 32, size_y * 32, size_x, size_y),
    )


def masses_of(density, copies):
    return pl.pallas_call(
        masses_kernel,
        out_shape=shape(copies, 64, 128),
        in_specs=[VMEM],
        out_specs=VMEM,
        compiler_params=params(16),
        cost_estimate=cost(2e7, 1.2e6),
        name="masses",
    )(density)


def near_of(density, tables):
    strip = shape(4, 4, 8, 400)
    face = shape(8, 136, 128)
    return pl.pallas_call(
        near_kernel,
        out_shape=(shape(4, 4, 136, 400), strip, strip, face, face),
        in_specs=[SMEM] + [VMEM] * 9 + [pl.BlockSpec(memory_space=pl.ANY)],
        out_specs=(VMEM,) * 5,
        scratch_shapes=[
            pltpu.VMEM((NG, 4, 4, 8, 256), f32),
            pltpu.VMEM((NR, 3, 32, 384), f32),
            pltpu.VMEM((NC, 4, 32, 512), f32),
            pltpu.VMEM((4, 4, 304, 512), f32),
            pltpu.VMEM((PATCH, 64, 128), b16),
            pltpu.VMEM((RING, 2, ROWS, 256), b16),
            pltpu.SemaphoreType.DMA((RING,)),
        ],
        compiler_params=params(54),
        cost_estimate=cost(8e9, 5e7),
        name="near",
    )(
        tables["weights"],
        density,
        tables["forward"],
        tables["mirror"],
        tables["gather"],
        tables["coarse"],
        tables["backward"],
        *tables["swap"],
        tables["dense"],
    )


def inner_of(wide, from_lower, from_upper, tables):
    return pl.pallas_call(
        inner_kernel,
        out_shape=(
            shape(24, 136, 256),
            shape(24, 8, 256),
            shape(24, 8, 256),
            shape(2, 8, 120, 256),
        ),
        in_specs=[VMEM] * 4,
        out_specs=(VMEM,) * 4,
        scratch_shapes=[pltpu.VMEM((2, 8, 400, 256), f32)],
        compiler_params=params(28),
        cost_estimate=cost(5e9, 1e7),
        name="inner",
    )(wide, from_lower, from_upper, tables["unfold"])


def outer_of(outer, from_below, from_above, corner_lower, corner_upper, tables):
    return pl.pallas_call(
        outer_kernel,
        out_shape=(shape(12, 136, 256), shape(12, 8, 256), shape(12, 8, 256)),
        in_specs=[VMEM] * 6,
        out_specs=(VMEM,) * 3,
        scratch_shapes=[pltpu.VMEM((2, 8, 128, 256), f32)],
        compiler_params=params(16),
        cost_estimate=cost(4e9, 5e6),
        name="outer",
    )(outer, from_below, from_above, corner_lower, corner_upper, tables["unfold"])


def planes_of(far, tables):
    return pl.pallas_call(
        planes_kernel,
        out_shape=shape(REACH, 136, 256),
        in_specs=[VMEM] * 3,
        out_specs=VMEM,
        compiler_params=params(12),
        cost_estimate=cost(3e9, 2e6),
        name="planes",
    )(far, *tables["far"][6:])


def far_of(where, masses, tables):
    along_y, along_x, column, back_x, back_y, even = tables["far"][:6]
    parts = along_x.shape[0] * along_y.shape[0]
    total = masses.shape[0] * CQ

    def fixed(*dims):
        return pl.BlockSpec(dims, lambda i, w: (0,) * len(dims))

    return pl.pallas_call(
        far_kernel,
        grid_spec=pltpu.PrefetchScalarGridSpec(
            num_scalar_prefetch=1,
            grid=(1,),
            in_specs=[
                fixed(*masses.shape),
                pl.BlockSpec((1, 2, 128, 512), lambda i, w: (w[1], 0, 0, 0)),
                pl.BlockSpec((1, 128, 96), lambda i, w: (w[0], 0, 0)),
                fixed(*column.shape),
                fixed(*back_x.shape),
                fixed(*back_y.shape),
                fixed(*even.shape),
            ],
            out_specs=fixed(parts, 40, LANES),
            scratch_shapes=[
                pltpu.VMEM((total, 128, 128), f32),
                pltpu.VMEM((REACH, 128, 128), f32),
                pltpu.VMEM((4, LANES, 128), f32),
            ],
        ),
        out_shape=shape(parts, 40, LANES),
        compiler_params=params(48),
        cost_estimate=cost(4e9, 9e6),
        name="far",
    )(where, masses, along_y, along_x, column, back_x, back_y, even)


def final_of(inner, outer, planes):
    depth = 4
    operands = (*inner, *outer, planes)
    return pl.pallas_call(
        functools.partial(final_kernel, depth=depth),
        grid=(PATCH // depth,),
        out_shape=(shape(PATCH, 128, 128), shape(3, PATCH, 128, 128, dtype=b16)),
        in_specs=[pl.BlockSpec(values.shape, lambda i: (0, 0, 0)) for values in operands],
        out_specs=(
            pl.BlockSpec((depth, 128, 128), lambda i: (i, 0, 0)),
            pl.BlockSpec((3, depth, 128, 128), lambda i: (0, i, 0, 0)),
        ),
        scratch_shapes=[pltpu.VMEM((36, 136, 256), f32)],
        compiler_params=params(32),
        cost_estimate=cost(2e8, 1.2e7),
        name="final",
    )(*operands)


def moved(values, **steps):
    axes = tuple(steps)
    sizes = [lax.axis_size(axis) for axis in axes]
    pairs = []
    for source in np.ndindex(*sizes):
        target = [(i + step) % size for i, step, size in zip(source, steps.values(), sizes)]
        pairs.append(
            (int(np.ravel_multi_index(source, sizes)), int(np.ravel_multi_index(target, sizes)))
        )
    return lax.ppermute(values, axes, pairs)


def body(tables, density):
    size_gz = lax.axis_size("gz")
    where = jnp.stack([lax.axis_index(axis) for axis in ("gx", "gy", "gz")]).astype(jnp.int32)
    masses = masses_of(density, size_gz)
    masses = lax.all_to_all(masses, "gz", 0, 0, tiled=True)
    wide, upper, lower, bottom, top = near_of(density, tables)
    from_below = moved(top, gz=1)
    from_above = moved(bottom, gz=-1)
    from_lower = moved(upper, gy=1).reshape(2, 8, 8, 400)
    from_upper = moved(lower, gy=-1).reshape(2, 8, 8, 400)
    far = far_of(where, masses, tables)
    far = lax.all_to_all(far, ("gx", "gy"), 0, 0, tiled=True)
    faces = jnp.stack([from_below, from_above])
    corner_lower = moved(jnp.concatenate([faces[:, :, 128:132], faces[:, :, 124:128]], axis=2), gy=1)
    corner_upper = moved(jnp.concatenate([faces[:, :, 0:4], faces[:, :, 132:136]], axis=2), gy=-1)
    wide = wide.reshape(2, 8, 136, 400)
    near, upper, lower, outer = inner_of(wide, from_lower, from_upper, tables)
    inner = (near, moved(upper, gx=1), moved(lower, gx=-1))
    near, upper, lower = outer_of(
        outer, from_below, from_above, corner_lower, corner_upper, tables
    )
    outer = (near, moved(upper, gx=1), moved(lower, gx=-1))
    return final_of(inner, outer, planes_of(far, tables))


def solution(mesh):
    tables = make_tables(mesh.shape["gz"], mesh.shape["gx"], mesh.shape["gy"])
    return jax.shard_map(
        functools.partial(body, tables),
        mesh=mesh,
        in_specs=(P("gz", "gx", "gy"),),
        out_specs=(P("gz", "gx", "gy"), P(None, "gz", "gx", "gy")),
        check_vma=False,
    )
```

```python
import functools
import math

import jax
import jax.numpy as jnp
import ml_dtypes
import numpy as np
from jax import lax
from jax.experimental import pallas as pl
from jax.experimental.pallas import tpu as pltpu
from jax.sharding import PartitionSpec as P

HOCK = 72
RATIO = 4
PATCH = 32
CQ = 8
CH = HOCK // RATIO
NF = HOCK // 2 + 1
NC = CH // 2 + 1
NG = 48
NR = 40
RING = 16
ROWS = 1056
PAIRS = 320

f32 = jnp.float32
b16 = jnp.bfloat16
MIB = 1 << 20


def halves(table):
    high = table.astype(ml_dtypes.bfloat16)
    low = (table - high.astype(np.float64)).astype(ml_dtypes.bfloat16)
    return high, low


def centred(length, cells, centre):
    freq = np.arange(length // 2 + 1)
    weight = np.where((freq == 0) | (freq == length // 2), 1.0, 2.0)
    angle = 2.0 * math.pi / length * freq[:, None] * (cells - centre)[None, :]
    basis = np.stack([np.cos(angle), np.sin(angle)], axis=1)
    basis *= np.sqrt(weight / length)[:, None, None]
    return np.where(np.abs(basis) < 1e-12, 0.0, basis)


def fine_basis(cells):
    return centred(HOCK, cells, (PATCH - 1) / 2)


def coarse_basis(cells):
    return centred(CH, cells, (CQ - 1) / 2)


def inverse_distance(square, ratio):
    return np.where(
        square > 0, 1.0 / (4.0 * math.pi * ratio * np.sqrt(np.maximum(square, 1))), 0.25 / ratio
    )


def line_spectra(length, reach, ratio):
    index = np.arange(length)
    wrap = np.minimum(index, length - index)
    side = np.arange(reach)
    square = side[:, None, None] ** 2 + side[None, :, None] ** 2 + wrap[None, None, :] ** 2
    kernel = inverse_distance(square, ratio)
    cosine = np.cos(2.0 * math.pi / length * np.outer(np.arange(length // 2 + 1), index))
    return np.einsum("fd,abd->fab", cosine, kernel)


def refine_table(fine, coarse):
    return np.maximum(0.0, 1.0 - np.abs((fine[:, None] + 0.5) / RATIO - 0.5 - coarse[None, :]))


def sign(odd, mirrored):
    return -1.0 if (odd and mirrored) else 1.0


def swap_pairs(count):
    first, second = np.triu_indices(count)
    above, beyond = np.triu_indices(count, 1)
    return (first, second), (above, beyond)


def dense_table():
    spectra = line_spectra(HOCK, 36, 1)
    target = np.arange(20)[None, :] - RATIO
    source = np.arange(16)[:, None]
    near, far = np.abs(target - source), np.abs(target - (PATCH - 1 - source))

    def pick(first, second):
        return spectra[:, first[:, None, :, None], second[None, :, None, :]]

    terms = {(a, b): pick((near, far)[a], (near, far)[b]) for a in (0, 1) for b in (0, 1)}
    table = np.zeros((NF, ROWS, 256))
    for parity in range(4):
        odd_z, odd_x = divmod(parity, 2)
        if parity == 2:
            continue
        total = sum(sign(odd_z, a) * sign(odd_x, b) * terms[a, b] for a in (0, 1) for b in (0, 1))
        total = 0.25 * total
        if parity == 1:
            flat = total.reshape(NF, 256, 400)
            table[:, 544:800] = flat[:, :, :256]
            table[:, 800:1056, :144] = flat[:, :, 256:]
            continue
        base = 0 if parity == 0 else 272
        whole_in, strict_in = swap_pairs(16)
        whole_out, strict_out = swap_pairs(20)
        swapped = total.transpose(0, 2, 1, 3, 4)
        both, less = 0.5 * (total + swapped), 0.5 * (total - swapped)
        table[:, base : base + 136, :210] = both[:, whole_in[0], whole_in[1]][
            :, :, whole_out[0], whole_out[1]
        ]
        table[:, base + 144 : base + 264, :190] = less[:, strict_in[0], strict_in[1]][
            :, :, strict_out[0], strict_out[1]
        ]
    result = np.empty((NF, 2, ROWS, 256), ml_dtypes.bfloat16)
    result[:, 0], result[:, 1] = halves(table)
    return result


def swap_tables():
    whole, strict = swap_pairs(16)
    inward = np.zeros((16, 16, 384))
    spots = np.arange(136)
    inward[whole[0], whole[1], spots] = 1.0
    inward[whole[1], whole[0], spots] = 1.0
    spots = 256 + np.arange(120)
    inward[strict[0], strict[1], spots] = 1.0
    inward[strict[1], strict[0], spots] = -1.0
    whole, strict = swap_pairs(20)
    outward = np.zeros((2, 512, 20, 20))
    spots = np.arange(210)
    outward[0, spots, whole[0], whole[1]] = 1.0
    outward[0, spots, whole[1], whole[0]] = 1.0
    spots = 256 + np.arange(190)
    outward[0, spots, strict[0], strict[1]] = 1.0
    outward[0, spots, strict[1], strict[0]] = -1.0
    outward[1, :400] = np.eye(400).reshape(20, 20, 20, 20).transpose(1, 0, 2, 3).reshape(400, 20, 20)
    turn = np.eye(256).reshape(16, 16, 16, 16).transpose(1, 0, 2, 3).reshape(256, 256)
    return tuple(
        table.astype(ml_dtypes.bfloat16)
        for table in (inward.reshape(256, 384), turn, outward.reshape(2, 512, 400))
    )


def coarse_dense_table():
    spectra = line_spectra(CH, 10, RATIO)
    window = np.arange(-2, CQ + 2)
    apart = np.abs(window[:, None] - np.arange(CQ)[None, :])
    kernel = spectra[:, apart[:, None, :, None], apart[None, :, None, :]]
    spread = refine_table(np.arange(20) - RATIO, window)
    kernel = np.einsum("za,xb,fabcd->fcdzx", spread, spread, kernel)
    whole, strict = swap_pairs(20)
    result = np.empty((NC, 4, 2, 16, 512), ml_dtypes.bfloat16)
    for parity in range(4):
        odd_z, odd_x = divmod(parity, 2)
        mirrored = kernel[:, ::-1]
        total = kernel + (-1.0) ** odd_z * mirrored
        total = total + (-1.0) ** odd_x * total[:, :, ::-1]
        total = 0.25 * total[:, :4, :4].reshape(NC, 16, 20, 20)
        swapped = total.transpose(0, 1, 3, 2)
        table = np.zeros((NC, 16, 512))
        if parity == 1:
            table[:, :, :400] = total.reshape(NC, 16, 400)
        elif parity == 2:
            table[:, :, :400] = swapped.reshape(NC, 16, 400)
        else:
            table[:, :, :210] = (0.5 * (total + swapped))[:, :, whole[0], whole[1]]
            table[:, :, 256:446] = (0.5 * (total - swapped))[:, :, strict[0], strict[1]]
        result[:, parity, 0], result[:, parity, 1] = halves(table)
    return result


def forward_table():
    cells = np.arange(PATCH)
    lines = np.zeros((NG, 2, PATCH))
    lines[:NF] = fine_basis(cells)
    lines[NF : NF + NC] = coarse_basis(cells // RATIO)
    table = np.zeros((NG, 2, 4, 4, PATCH))
    for patch in range(4):
        table[:, :, patch, patch] = lines
    high, low = halves(table.reshape(4, 96, 128))
    return np.concatenate([high, low], axis=1)


def mirror_table():
    table = np.zeros((64, 128))
    for patch in range(4):
        for cell in range(16):
            table[patch * 16 + cell, patch * 32 + 31 - cell] = 1.0
    return table.astype(ml_dtypes.bfloat16)


def gather_table():
    table = np.zeros((16, 16, 4, 4))
    for z in range(16):
        for x in range(16):
            table[z, x, z // RATIO, x // RATIO] = 1.0
    return table.reshape(256, 16).astype(ml_dtypes.bfloat16)


def alias_weights():
    fine = np.arange(HOCK)
    spread = np.zeros((HOCK, CH))
    for shift in (-1, 0, 1):
        spread += refine_table(fine, np.arange(CH) + shift * CH)
    mapped = np.einsum("fct,tY,GcY->fcG", fine_basis(fine), spread, coarse_basis(np.arange(CH)))
    rest = np.arange(NF) % CH
    alias = np.minimum(rest, CH - rest)
    return mapped[np.arange(NF), :, alias]


BLOCK = 128
BEYOND = [128, 129, 130, 131, -4, -3, -2, -1]
UPPER = [128, 129, 130, 131, 124, 125, 126, 127]
LOWER = [0, 1, 2, 3, -4, -3, -2, -1]
PLACES = np.array(list(range(BLOCK)) + BEYOND + UPPER + LOWER)


def backward_table():
    table = np.zeros((160, 38, 2, 4))
    for patch in range(4):
        cells = PLACES - PATCH * patch
        inside = (cells >= -RATIO) & (cells < PATCH + RATIO)
        values = fine_basis(cells) * inside
        table[:152, :NF, :, patch] = values.transpose(2, 0, 1)
    high, low = halves(table.reshape(160, 304))
    return np.concatenate([high, high, low], axis=1)


def unfold_table():
    table = np.zeros((2, 2, 160, 2, 4, 2, 20))
    for odd in range(2):
        for patch in range(4):
            for row, place in enumerate(PLACES):
                cell = place - PATCH * patch + RATIO
                if 0 <= cell < 20:
                    column, value = cell, 1.0
                elif 20 <= cell < 40:
                    column, value = 39 - cell, sign(odd, 1)
                else:
                    continue
                for layer in range(2):
                    table[0, layer, row, odd, patch, layer, column] = value
                    table[1, layer, row, odd, patch, 1 - layer, column] = value
    return table.reshape(2, PAIRS, 320).astype(ml_dtypes.bfloat16)


def periodic_basis(length, cells):
    slots = np.arange(length)
    freq = np.where(slots <= length // 2, slots, slots - length // 2)
    weight = np.where((freq == 0) | (freq == length // 2), 1.0, 2.0)
    angle = 2.0 * math.pi / length * (freq[:, None] * cells[None, :] % length)
    basis = np.where((slots <= length // 2)[:, None], np.cos(angle), np.sin(angle))
    return basis * np.sqrt(weight / length)[:, None], freq


REACH = CQ + 2
SIDE = 34
LANES = 384


def far_tables(total_z, total_x, total_y, parts_x, parts_y):
    basis_y, freq_y = periodic_basis(total_y, np.arange(total_y))
    basis_x, freq_x = periodic_basis(total_x, np.arange(total_x))
    along_y = np.zeros((parts_y, 4, 32, 4, total_y))
    for layer in range(4):
        along_y[:, layer, :, layer, :] = basis_y.T.reshape(parts_y, 32, total_y)
    along_y = np.stack(halves(along_y.reshape(parts_y, 128, 4 * total_y)), axis=1)
    high, low = halves(basis_x.reshape(total_x, parts_x, 32).transpose(1, 0, 2))
    along_x = np.concatenate([high, high, low], axis=2)

    def eigen(freq, length):
        return 2.0 - 2.0 * np.cos(2.0 * math.pi / length * freq)

    freq_z = np.arange(total_z)
    square = (
        eigen(freq_z, total_z)[:, None, None]
        + eigen(freq_x, total_x)[None, :, None]
        + eigen(freq_y, total_y)[None, None, :]
    )
    square[0, 0, 0] = 1.0
    inverse = 1.0 / (RATIO * square)
    inverse[0, 0, 0] = 0.0
    steps = np.arange(total_z // 2 + 1)
    cosine = np.cos(2.0 * math.pi / total_z * np.outer(steps, freq_z)) / total_z
    column = np.einsum("dk,kxy->dxy", cosine, inverse).astype(np.float32)

    def windows(length, parts, basis):
        table = np.zeros((parts, 40, length))
        for part in range(parts):
            cells = (np.arange(SIDE) - 1 + part * 32) % length
            table[part, :SIDE] = basis[:, cells].T
        return table.reshape(parts * 40, length)

    square = eigen(freq_x, total_x)[:, None] + eigen(freq_y, total_y)[None, :]
    square[0, 0] = 1.0
    inverse = 1.0 / (RATIO * square)
    inverse[0, 0] = 0.0
    weight = np.outer(basis_x[:, :32].sum(axis=1), basis_y[:, :32].sum(axis=1)) * inverse
    flat = basis_x.T @ weight @ basis_y
    even = np.zeros((parts_x, parts_y, 40, LANES))
    for part in range(parts_x):
        cells_x = (np.arange(SIDE) - 1 + part * 32) % total_x
        for other in range(parts_y):
            cells_y = (np.arange(SIDE) - 1 + other * 32) % total_y
            values = flat[cells_x][:, cells_y].T
            even[part, other, :SIDE, : REACH * SIDE] = np.tile(values, (1, REACH))
    even = even.reshape(parts_x * parts_y, 40, LANES).astype(np.float32)

    back_x = np.concatenate(halves(windows(total_x, parts_x, basis_x)), axis=1)
    back_y = np.stack(halves(windows(total_y, parts_y, basis_y)))
    return along_y, along_x, column, back_x, back_y, even


def parts_of(values):
    high = values.astype(b16)
    return high, (values - high.astype(f32)).astype(b16)


def mul(left, right):
    return jnp.dot(left, right, preferred_element_type=f32)


def mul_nt(left, right):
    return lax.dot_general(left, right, (((1,), (1,)), ((), ())), preferred_element_type=f32)


def masses_kernel(rho_ref, out_ref):
    row = lax.broadcasted_iota(jnp.int32, (32, 512), 0)
    column = lax.broadcasted_iota(jnp.int32, (32, 512), 1)
    sum_x = jnp.where(column % 128 // RATIO == row, 1.0, 0.0).astype(b16)
    row = lax.broadcasted_iota(jnp.int32, (128, 128), 0)
    column = lax.broadcasted_iota(jnp.int32, (128, 128), 1)
    for half in range(2):
        total = jnp.zeros((32, 128), f32)
        for layer in range(4):
            z = (half * 4 + layer) * RATIO
            slab = rho_ref[pl.ds(z, RATIO)].reshape(RATIO * 128, 128)
            rows = mul(sum_x, slab)
            high, rest = parts_of(rows)
            mid, low = parts_of(rows - high.astype(f32))
            weights = jnp.where(row // RATIO + layer * 32 == column, 1.0, 0.0).astype(b16)
            total += mul(high, weights) + (mul(mid, weights) + mul(low, weights))
        for copy in range(out_ref.shape[0]):
            out_ref[copy, half * 32 : half * 32 + 32, :] = total


def mul_pairs(values, high_table, low_table):
    rows = values.shape[0]
    high, low = parts_of(values)
    both = mul(jnp.concatenate([high, low], axis=0), high_table)
    return both[:rows] + (both[rows:] + mul(high, low_table))


def mul_exact(values, table):
    rows = values.shape[0]
    high, low = parts_of(values)
    both = mul(jnp.concatenate([high, low], axis=0), table)
    return both[:rows] + both[rows:]


def near_kernel(
    weights_ref,
    rho_ref,
    forward_ref,
    mirror_ref,
    gather_ref,
    coarse_ref,
    backward_ref,
    inward_ref,
    turn_ref,
    outward_ref,
    dense_ref,
    wide_ref,
    upper_ref,
    lower_ref,
    bottom_ref,
    top_ref,
    lines,
    ready,
    smooth,
    spectra,
    turned,
    ring,
    arrived,
):
    def fetch(freq, slot):
        return pltpu.make_async_copy(dense_ref.at[freq], ring.at[slot], arrived.at[slot])

    for slot in range(RING):
        fetch(slot, slot).start()

    for z in range(PATCH):
        turned[z] = mul(mirror_ref[...], rho_ref[z]).astype(b16)
    for patch in range(4):
        def rows(mirror_z, mirror_x):
            tiles = []
            for z in range(16):
                layer = PATCH - 1 - z if mirror_z else z
                if mirror_x:
                    tiles.append(turned[layer, patch * 16 : patch * 16 + 16, :])
                else:
                    tiles.append(rho_ref[layer, patch * 32 : patch * 32 + 16, :])
            return jnp.concatenate(tiles, axis=0)

        right = [rows(0, 0), rows(0, 1), rows(1, 0), rows(1, 1)]

        def chunk(index):
            left = forward_ref[index]
            sums = []
            for mirror in range(4):
                both = mul_nt(left, right[mirror])
                sums.append(both[:96] + both[96:])
            even, odd = sums[0] + sums[1], sums[0] - sums[1]
            even_far, odd_far = sums[2] + sums[3], sums[2] - sums[3]
            freqs = slice(index * 12, index * 12 + 12)
            lines[freqs, 0, patch] = (even + even_far).reshape(12, 8, 256)
            lines[freqs, 1, patch] = (odd + odd_far).reshape(12, 8, 256)
            lines[freqs, 2, patch] = (even - even_far).reshape(12, 8, 256)
            lines[freqs, 3, patch] = (odd - odd_far).reshape(12, 8, 256)

        for index in range(4):
            chunk(index)

    for parity in range(4):
        values = lines[NF : NF + NC, parity].reshape(NC * 32, 256)
        high, low = parts_of(mul_exact(values, gather_ref[...]))
        for freq in range(NC):
            both = jnp.concatenate(
                [high[freq * 32 : freq * 32 + 32], low[freq * 32 : freq * 32 + 32]], axis=0
            )
            value = mul(both, coarse_ref[freq, parity, 0])
            smooth[freq, parity] = value[:32] + (
                value[32:] + mul(both[:32], coarse_ref[freq, parity, 1])
            )

    def prepare(index):
        freqs = pl.ds(index * 4, 4)
        for slot, parity in ((0, 0), (1, 3)):
            values = lines[freqs, parity].reshape(128, 256)
            ready[freqs, slot] = mul_exact(values, inward_ref[...]).reshape(4, 32, 384)
        values = lines[freqs, 2].reshape(128, 256)
        ready[freqs, 2, :, 0:256] = mul_exact(values, turn_ref[...]).reshape(4, 32, 256)

    def prepare_two(index, carry):
        prepare(2 * index)
        prepare(2 * index + 1)
        return carry

    lax.fori_loop(0, NR // 8, prepare_two, 0)
    spectra[:, :, 8 * NF :, :] = jnp.zeros((4, 4, 8, 512), f32)
    row = lax.broadcasted_iota(jnp.int32, (32, 1), 0)

    def solve(freq):
        slot = lax.rem(freq, RING)
        fetch(freq, slot).wait()
        rest = lax.rem(freq, CH)
        alias = jnp.minimum(rest, CH - rest)
        weight = jnp.where(row % 8 < 4, weights_ref[freq, 0], weights_ref[freq, 1])
        here = pl.ds(freq * 8, 8)

        def keep(parity, low, high, value):
            value = value - weight * smooth[alias, parity, :, low:high]
            spectra[parity, :, here, low:high] = value.reshape(4, 8, 256)

        for place, parity in ((0, 0), (1, 3)):
            for base, count, lane in ((0, 144, 0), (144, 128, 256)):
                base = base + 272 * place
                value = mul_pairs(
                    ready[freq, place, :, lane : lane + count],
                    ring[slot, 0, base : base + count, :],
                    ring[slot, 1, base : base + count, :],
                )
                keep(parity, lane, lane + 256, value)
        values = jnp.concatenate(
            [lines[freq, 1].reshape(32, 256), ready[freq, 2, :, 0:256]], axis=0
        )
        for base, lane in ((544, 0), (800, 256)):
            value = mul_pairs(
                values, ring[slot, 0, base : base + 256, :], ring[slot, 1, base : base + 256, :]
            )
            keep(1, lane, lane + 256, value[:32])
            keep(2, lane, lane + 256, value[32:])

        @pl.when(freq + RING < NF)
        def _():
            fetch(freq + RING, slot).start()

    def solve_two(index, carry):
        solve(2 * index)
        solve(2 * index + 1)
        return carry

    lax.fori_loop(0, NF // 2, solve_two, 0)
    solve(jnp.int32(NF - 1))

    for parity in range(4):
        values = []
        for patch in range(4):
            high, low = parts_of(spectra[parity, patch])
            values.append(mul(backward_ref[...], jnp.concatenate([high, low, high], axis=0)))
        if parity != 1:
            pairs = [part for value in values for part in parts_of(value)]
            table = outward_ref[1 if parity == 2 else 0]
            both = mul(jnp.concatenate(pairs, axis=0), table)
            values = [
                both[320 * patch : 320 * patch + 160] + both[320 * patch + 160 : 320 * patch + 320]
                for patch in range(4)
            ]
        for patch in range(4):
            wide_ref[parity, patch] = values[patch][:136, :400]
            upper_ref[parity, patch] = values[patch][136:144, :400]
            lower_ref[parity, patch] = values[patch][144:152, :400]

    for odd_x in range(2):
        for patch in range(4):
            index = odd_x * 4 + patch
            even = wide_ref[odd_x, patch, :, 0:128]
            odd = wide_ref[2 + odd_x, patch, :, 0:128]
            bottom_ref[index] = even + odd
            top_ref[index] = even - odd


def with_neighbours(values, from_lower, from_upper):
    first = lax.broadcasted_iota(jnp.int32, from_lower.shape, 0) < 4
    zero = jnp.zeros_like(from_lower)
    return jnp.concatenate(
        [
            values[0:8] + jnp.where(first, from_lower, zero),
            values[8:120],
            values[120:128] + jnp.where(first, zero, from_upper),
            values[128:136] + jnp.where(first, from_upper, from_lower),
        ],
        axis=0,
    )


def turned_into(ref, side, index, value):
    ref[side, index, :, 0:128] = value[:128].T
    ref[side, index, :, 128:136] = value[128:136].T


def rows_of(ref, side, pair):
    rows = slice(40 * pair, 40 * pair + 40)
    return jnp.concatenate([ref[side, index, rows, :] for index in range(8)], axis=0)


def unfolded(table, rows):
    high, low = parts_of(rows)
    return mul(table, high) + mul(table, low)


def store_layers(value, places, near_ref, upper_ref, lower_ref):
    for layer, z in enumerate(places):
        near_ref[z] = value[160 * layer : 160 * layer + 136]
        upper_ref[z] = value[160 * layer + 136 : 160 * layer + 144]
        lower_ref[z] = value[160 * layer + 144 : 160 * layer + 152]


def inner_kernel(
    wide_hbm,
    from_lower_hbm,
    from_upper_hbm,
    unfold_ref,
    near_hbm,
    upper_ref,
    lower_ref,
    outer_hbm,
    standing,
    wide_ref,
    from_lower_ref,
    from_upper_ref,
    near_ref,
    arrived,
    written,
):
    def fetch(index):
        return pltpu.make_async_copy(wide_hbm.at[:, index], wide_ref.at[:, index], arrived.at[index])

    strips = [
        pltpu.make_async_copy(from_lower_hbm, from_lower_ref, arrived.at[8]),
        pltpu.make_async_copy(from_upper_hbm, from_upper_ref, arrived.at[9]),
    ]
    for strip in strips:
        strip.start()
    for index in range(8):
        fetch(index).start()
    for strip in strips:
        strip.wait()

    def turn(index, carry):
        fetch(index).wait()
        even = with_neighbours(wide_ref[0, index], from_lower_ref[0, index], from_upper_ref[0, index])
        odd = with_neighbours(wide_ref[1, index], from_lower_ref[1, index], from_upper_ref[1, index])
        turned_into(standing, 0, index, even + odd)
        turned_into(standing, 1, index, even - odd)
        return carry

    lax.fori_loop(0, 8, turn, 0)
    results = [pltpu.make_async_copy(standing.at[:, :, 40:160, :], outer_hbm, written.at[0])]
    results[0].start()
    for pair in range(4, 10):
        for side in range(2):
            value = unfolded(unfold_ref[0], rows_of(standing, side, pair))
            places = [2 * pair - 8, 2 * pair - 7]
            if side == 1:
                places = [23 - z for z in places]
            store_layers(value, places, near_ref, upper_ref, lower_ref)
            pieces = pl.ds(min(places), 2)
            results.append(
                pltpu.make_async_copy(
                    near_ref.at[pieces], near_hbm.at[pieces], written.at[len(results)]
                )
            )
            results[-1].start()
    for result in results:
        result.wait()


def outer_kernel(
    outer_ref,
    from_below_ref,
    from_above_ref,
    corner_lower_ref,
    corner_upper_ref,
    unfold_ref,
    near_ref,
    upper_ref,
    lower_ref,
    given,
):
    def turn(index, carry):
        for side, ref in ((0, from_below_ref), (1, from_above_ref)):
            value = with_neighbours(
                ref[index], corner_lower_ref[side, index], corner_upper_ref[side, index]
            )
            turned_into(given, side, index, value)
        return carry

    lax.fori_loop(0, 8, turn, 0)
    for pair in range(3):
        for side in range(2):
            value = unfolded(unfold_ref[0], rows_of(outer_ref, side, pair))
            value = value + unfolded(unfold_ref[1], rows_of(given, side, 2 - pair))
            places = [2 * pair, 2 * pair + 1]
            if side == 1:
                places = [11 - z for z in places]
            store_layers(value, places, near_ref, upper_ref, lower_ref)


def far_kernel(
    where_ref,
    masses_ref,
    along_y_ref,
    along_x_ref,
    column_hbm,
    back_x_ref,
    back_y_ref,
    even_hbm,
    out_ref,
    spectra,
    lines,
    turned,
    column_ref,
    even_ref,
    arrived,
):
    tables = [
        pltpu.make_async_copy(column_hbm, column_ref, arrived.at[0]),
        pltpu.make_async_copy(even_hbm, even_ref, arrived.at[1]),
    ]
    for table in tables:
        table.start()
    blocks = masses_ref.shape[0]
    total = spectra.shape[0]
    masses = masses_ref[...].reshape(blocks * 64, 128)
    mean = jnp.sum(masses, axis=(0, 1), keepdims=True) * (1.0 / masses.size)
    high, low = parts_of(masses - mean)
    value = mul(high, along_y_ref[0, 0]) + (
        mul(low, along_y_ref[0, 0]) + mul(high, along_y_ref[0, 1])
    )
    high, low = parts_of(value)
    for half in range(2 * blocks):
        rows = slice(half * 32, half * 32 + 32)
        right = jnp.concatenate([high[rows], low[rows], high[rows]], axis=0)
        value = mul(along_x_ref[0], right)
        for layer in range(4):
            spectra[half * 4 + layer] = value[:, layer * 128 : layer * 128 + 128]

    start = where_ref[2] * CQ
    for table in tables:
        table.wait()

    def solve(tile, carry):
        rows = pl.ds(pl.multiple_of(tile * 8, 8), 8)
        sums = [jnp.zeros((8, 128), f32) for _ in range(REACH)]
        for step in range(total):
            value = spectra[lax.rem(start + step, total), rows, :]
            for layer in range(REACH):
                apart = abs(step - (layer - 1)) % total
                sums[layer] += value * column_ref[min(apart, total - apart), rows, :]
        for layer in range(REACH):
            lines[layer, rows, :] = sums[layer]
        return carry

    lax.fori_loop(0, 16, solve, 0)

    turned[:, REACH * SIDE :, :] = jnp.zeros((4, LANES - REACH * SIDE, 128), f32)
    for layer in range(REACH):
        high, low = parts_of(lines[layer])
        value = mul(back_x_ref[:, 0:128], high) + (
            mul(back_x_ref[:, 0:128], low) + mul(back_x_ref[:, 128:256], high)
        )
        for part in range(4):
            turned[part, layer * SIDE : layer * SIDE + SIDE, :] = value[part * 40 : part * 40 + SIDE]
    for part in range(4):
        high, low = parts_of(turned[part])
        value = mul_nt(back_y_ref[0], high) + (
            mul_nt(back_y_ref[0], low) + mul_nt(back_y_ref[1], high)
        )
        for other in range(4):
            apart = lax.rem(part + 4 - where_ref[0], 4) * 4 + lax.rem(other + 4 - where_ref[1], 4)
            out_ref[part * 4 + other] = value[other * 40 : other * 40 + 40] + mean * even_ref[apart]


def share(fine, coarse):
    fine = jnp.where(fine < 132, fine, fine - 136).astype(f32)
    return jnp.maximum(0.0, 1.0 - jnp.abs((fine + 0.5) / RATIO - 0.5 - coarse.astype(f32)))


def planes_kernel(far_ref, out_ref):
    sums = far_ref[0]
    for source in range(1, far_ref.shape[0]):
        sums = sums + far_ref[source]
    right = jnp.concatenate(parts_of(sums), axis=0)
    row = lax.broadcasted_iota(jnp.int32, (136, LANES), 0)
    lane = lax.broadcasted_iota(jnp.int32, (136, LANES), 1)
    spread_x = []
    for layer in range(REACH):
        coarse = lane - layer * SIDE
        inside = (coarse >= 0) & (coarse < SIDE)
        spread_x.append(jnp.where(inside, share(row, coarse - 1), 0.0).astype(b16))
    value = mul_nt(jnp.concatenate(spread_x, axis=0), right)
    first, second = parts_of(value[:, :40] + value[:, 40:])
    row = lax.broadcasted_iota(jnp.int32, (40, 256), 0)
    lane = lax.broadcasted_iota(jnp.int32, (40, 256), 1)
    spread_y = jnp.where(row < SIDE, share(lane, row - 1), 0.0).astype(b16)
    value = mul(first, spread_y) + mul(second, spread_y)
    for layer in range(REACH):
        out_ref[layer] = value[layer * 136 : layer * 136 + 136]


def final_kernel(
    inner_ref,
    inner_lower_ref,
    inner_upper_ref,
    outer_ref,
    outer_lower_ref,
    outer_upper_ref,
    planes_ref,
    potential_ref,
    force_ref,
    whole,
    depth,
):
    step = pl.program_id(0)

    @pl.when(step == 0)
    def _():
        for z in range(36):
            place = (z - 2 + 0.5) / RATIO - 0.5
            below = math.floor(place)
            part = place - below
            if 6 <= z < 30:
                refs, spot = (inner_ref, inner_lower_ref, inner_upper_ref), z - 6
            else:
                refs, spot = (outer_ref, outer_lower_ref, outer_upper_ref), z % 24
            value = with_neighbours(*(ref[spot] for ref in refs))
            whole[z] = value + (
                (1.0 - part) * planes_ref[below + 1] + part * planes_ref[below + 2]
            )

    row = lax.broadcasted_iota(jnp.int32, (128, 128), 0)
    lane = lax.broadcasted_iota(jnp.int32, (128, 128), 1)

    def difference(plus_one, minus_one, plus_two, minus_two):
        value = -(2.0 / 3.0 * (plus_one - minus_one) - 1.0 / 12.0 * (plus_two - minus_two))
        return value.astype(b16)

    def beyond(values, edge, mask, shift, axis):
        return pltpu.roll(jnp.where(mask, edge, values), shift, axis)

    for inner in range(depth):
        z = step * depth + inner + 2
        here = whole[z, 0:128, 0:128]
        potential_ref[inner] = here
        force_ref[0, inner] = difference(
            whole[z + 1, 0:128, 0:128],
            whole[z - 1, 0:128, 0:128],
            whole[z + 2, 0:128, 0:128],
            whole[z - 2, 0:128, 0:128],
        )
        edge = whole[z, 128:136, 0:128]
        above = jnp.concatenate([edge, here[8:]], axis=0)
        below = jnp.concatenate([here[:120], edge], axis=0)
        force_ref[1, inner] = difference(
            beyond(here, above, row < 1, 127, 0),
            beyond(here, below, row >= 127, 1, 0),
            beyond(here, above, row < 2, 126, 0),
            beyond(here, below, row >= 126, 2, 0),
        )
        above = whole[z, 0:128, 128:256]
        below = pltpu.roll(above, 120, 1)
        force_ref[2, inner] = difference(
            beyond(here, above, lane < 1, 127, 1),
            beyond(here, below, lane >= 127, 1, 1),
            beyond(here, above, lane < 2, 126, 1),
            beyond(here, below, lane >= 126, 2, 1),
        )


VMEM = pl.BlockSpec(memory_space=pltpu.VMEM)
HBM = pl.BlockSpec(memory_space=pltpu.HBM)
SMEM = pl.BlockSpec(memory_space=pltpu.SMEM)


def params(size):
    return pltpu.CompilerParams(vmem_limit_bytes=size * MIB)


def cost(flops, moved):
    return pl.CostEstimate(flops=int(flops), bytes_accessed=int(moved), transcendentals=0)


def shape(*dims, dtype=f32):
    return jax.ShapeDtypeStruct(dims, dtype)


def make_tables(size_z, size_x, size_y):
    return dict(
        weights=alias_weights().astype(np.float32),
        forward=forward_table(),
        mirror=mirror_table(),
        gather=gather_table(),
        coarse=coarse_dense_table(),
        backward=backward_table(),
        dense=dense_table(),
        swap=swap_tables(),
        unfold=unfold_table(),
        far=far_tables(size_z * CQ, size_x * 32, size_y * 32, size_x, size_y),
    )


def masses_of(density, copies):
    return pl.pallas_call(
        masses_kernel,
        out_shape=shape(copies, 64, 128),
        in_specs=[VMEM],
        out_specs=VMEM,
        compiler_params=params(16),
        cost_estimate=cost(2e7, 1.2e6),
        name="masses",
    )(density)


def near_of(density, tables):
    strip = shape(4, 4, 8, 400)
    face = shape(8, 136, 128)
    return pl.pallas_call(
        near_kernel,
        out_shape=(shape(4, 4, 136, 400), strip, strip, face, face),
        in_specs=[SMEM] + [VMEM] * 9 + [pl.BlockSpec(memory_space=pl.ANY)],
        out_specs=(VMEM,) * 5,
        scratch_shapes=[
            pltpu.VMEM((NG, 4, 4, 8, 256), f32),
            pltpu.VMEM((NR, 3, 32, 384), f32),
            pltpu.VMEM((NC, 4, 32, 512), f32),
            pltpu.VMEM((4, 4, 304, 512), f32),
            pltpu.VMEM((PATCH, 64, 128), b16),
            pltpu.VMEM((RING, 2, ROWS, 256), b16),
            pltpu.SemaphoreType.DMA((RING,)),
        ],
        compiler_params=params(54),
        cost_estimate=cost(8e9, 5e7),
        name="near",
    )(
        tables["weights"],
        density,
        tables["forward"],
        tables["mirror"],
        tables["gather"],
        tables["coarse"],
        tables["backward"],
        *tables["swap"],
        tables["dense"],
    )


def inner_of(wide, from_lower, from_upper, tables):
    return pl.pallas_call(
        inner_kernel,
        out_shape=(
            shape(24, 136, 256),
            shape(24, 8, 256),
            shape(24, 8, 256),
            shape(2, 8, 120, 256),
        ),
        in_specs=[HBM] * 3 + [VMEM],
        out_specs=(HBM, VMEM, VMEM, HBM),
        scratch_shapes=[
            pltpu.VMEM((2, 8, 400, 256), f32),
            pltpu.VMEM((2, 8, 136, 400), f32),
            pltpu.VMEM((2, 8, 8, 400), f32),
            pltpu.VMEM((2, 8, 8, 400), f32),
            pltpu.VMEM((24, 136, 256), f32),
            pltpu.SemaphoreType.DMA((10,)),
            pltpu.SemaphoreType.DMA((13,)),
        ],
        compiler_params=params(60),
        cost_estimate=cost(5e9, 1e7),
        name="inner",
    )(wide, from_lower, from_upper, tables["unfold"])


def outer_of(outer, from_below, from_above, corner_lower, corner_upper, tables):
    return pl.pallas_call(
        outer_kernel,
        out_shape=(shape(12, 136, 256), shape(12, 8, 256), shape(12, 8, 256)),
        in_specs=[VMEM] * 6,
        out_specs=(VMEM,) * 3,
        scratch_shapes=[pltpu.VMEM((2, 8, 128, 256), f32)],
        compiler_params=params(16),
        cost_estimate=cost(4e9, 5e6),
        name="outer",
    )(outer, from_below, from_above, corner_lower, corner_upper, tables["unfold"])


def planes_of(far):
    return pl.pallas_call(
        planes_kernel,
        out_shape=shape(REACH, 136, 256),
        in_specs=[VMEM],
        out_specs=VMEM,
        compiler_params=params(12),
        cost_estimate=cost(3e9, 2e6),
        name="planes",
    )(far)


def far_of(where, masses, tables):
    along_y, along_x, column, back_x, back_y, even = tables["far"]
    parts = along_x.shape[0] * along_y.shape[0]
    total = masses.shape[0] * CQ

    def fixed(*dims):
        return pl.BlockSpec(dims, lambda i, w: (0,) * len(dims))

    return pl.pallas_call(
        far_kernel,
        grid_spec=pltpu.PrefetchScalarGridSpec(
            num_scalar_prefetch=1,
            grid=(1,),
            in_specs=[
                fixed(*masses.shape),
                pl.BlockSpec((1, 2, 128, 512), lambda i, w: (w[1], 0, 0, 0)),
                pl.BlockSpec((1, 128, 96), lambda i, w: (w[0], 0, 0)),
                HBM,
                fixed(*back_x.shape),
                fixed(*back_y.shape),
                HBM,
            ],
            out_specs=fixed(parts, 40, LANES),
            scratch_shapes=[
                pltpu.VMEM((total, 128, 128), f32),
                pltpu.VMEM((REACH, 128, 128), f32),
                pltpu.VMEM((4, LANES, 128), f32),
                pltpu.VMEM(column.shape, f32),
                pltpu.VMEM(even.shape, f32),
                pltpu.SemaphoreType.DMA((2,)),
            ],
        ),
        out_shape=shape(parts, 40, LANES),
        compiler_params=params(60),
        cost_estimate=cost(4e9, 9e6),
        name="far",
    )(where, masses, along_y, along_x, column, back_x, back_y, even)


def final_of(inner, outer, planes):
    depth = 4
    operands = (*inner, *outer, planes)
    return pl.pallas_call(
        functools.partial(final_kernel, depth=depth),
        grid=(PATCH // depth,),
        out_shape=(shape(PATCH, 128, 128), shape(3, PATCH, 128, 128, dtype=b16)),
        in_specs=[pl.BlockSpec(values.shape, lambda i: (0, 0, 0)) for values in operands],
        out_specs=(
            pl.BlockSpec((depth, 128, 128), lambda i: (i, 0, 0)),
            pl.BlockSpec((3, depth, 128, 128), lambda i: (0, i, 0, 0)),
        ),
        scratch_shapes=[pltpu.VMEM((36, 136, 256), f32)],
        compiler_params=params(26),
        cost_estimate=cost(2e8, 1.2e7),
        name="final",
    )(*operands)


def moved(values, **steps):
    axes = tuple(steps)
    sizes = [lax.axis_size(axis) for axis in axes]
    pairs = []
    for source in np.ndindex(*sizes):
        target = [(i + step) % size for i, step, size in zip(source, steps.values(), sizes)]
        pairs.append(
            (int(np.ravel_multi_index(source, sizes)), int(np.ravel_multi_index(target, sizes)))
        )
    return lax.ppermute(values, axes, pairs)


def body(tables, density):
    size_gz = lax.axis_size("gz")
    where = jnp.stack([lax.axis_index(axis) for axis in ("gx", "gy", "gz")]).astype(jnp.int32)
    masses = masses_of(density, size_gz)
    masses = lax.all_to_all(masses, "gz", 0, 0, tiled=True)
    wide, upper, lower, bottom, top = near_of(density, tables)
    from_below = moved(top, gz=1)
    from_above = moved(bottom, gz=-1)
    from_lower = moved(upper, gy=1).reshape(2, 8, 8, 400)
    from_upper = moved(lower, gy=-1).reshape(2, 8, 8, 400)
    far = far_of(where, masses, tables)
    far = lax.all_to_all(far, ("gx", "gy"), 0, 0, tiled=True)
    faces = jnp.stack([from_below, from_above])
    corner_lower = moved(jnp.concatenate([faces[:, :, 128:132], faces[:, :, 124:128]], axis=2), gy=1)
    corner_upper = moved(jnp.concatenate([faces[:, :, 0:4], faces[:, :, 132:136]], axis=2), gy=-1)
    wide = wide.reshape(2, 8, 136, 400)
    near, upper, lower, outer = inner_of(wide, from_lower, from_upper, tables)
    inner = (near, moved(upper, gx=1), moved(lower, gx=-1))
    near, upper, lower = outer_of(
        outer, from_below, from_above, corner_lower, corner_upper, tables
    )
    outer = (near, moved(upper, gx=1), moved(lower, gx=-1))
    return final_of(inner, outer, planes_of(far))


def solution(mesh):
    tables = make_tables(mesh.shape["gz"], mesh.shape["gx"], mesh.shape["gy"])
    return jax.shard_map(
        functools.partial(body, tables),
        mesh=mesh,
        in_specs=(P("gz", "gx", "gy"),),
        out_specs=(P("gz", "gx", "gy"), P(None, "gz", "gx", "gy")),
        check_vma=False,
    )
```

```python
import functools
import math

import jax
import jax.numpy as jnp
import ml_dtypes
import numpy as np
from jax import lax
from jax.experimental import pallas as pl
from jax.experimental.pallas import tpu as pltpu
from jax.sharding import PartitionSpec as P

HOCK = 72
RATIO = 4
PATCH = 32
CQ = 8
CH = HOCK // RATIO
NF = HOCK // 2 + 1
NC = CH // 2 + 1
NG = 48
NR = 40
RING = 16
ROWS = 1056
PAIRS = 320

f32 = jnp.float32
b16 = jnp.bfloat16
MIB = 1 << 20


def halves(table):
    high = table.astype(ml_dtypes.bfloat16)
    low = (table - high.astype(np.float64)).astype(ml_dtypes.bfloat16)
    return high, low


def centred(length, cells, centre):
    freq = np.arange(length // 2 + 1)
    weight = np.where((freq == 0) | (freq == length // 2), 1.0, 2.0)
    angle = 2.0 * math.pi / length * freq[:, None] * (cells - centre)[None, :]
    basis = np.stack([np.cos(angle), np.sin(angle)], axis=1)
    basis *= np.sqrt(weight / length)[:, None, None]
    return np.where(np.abs(basis) < 1e-12, 0.0, basis)


def fine_basis(cells):
    return centred(HOCK, cells, (PATCH - 1) / 2)


def coarse_basis(cells):
    return centred(CH, cells, (CQ - 1) / 2)


def inverse_distance(square, ratio):
    return np.where(
        square > 0, 1.0 / (4.0 * math.pi * ratio * np.sqrt(np.maximum(square, 1))), 0.25 / ratio
    )


def line_spectra(length, reach, ratio):
    index = np.arange(length)
    wrap = np.minimum(index, length - index)
    side = np.arange(reach)
    square = side[:, None, None] ** 2 + side[None, :, None] ** 2 + wrap[None, None, :] ** 2
    kernel = inverse_distance(square, ratio)
    cosine = np.cos(2.0 * math.pi / length * np.outer(np.arange(length // 2 + 1), index))
    return np.einsum("fd,abd->fab", cosine, kernel)


def refine_table(fine, coarse):
    return np.maximum(0.0, 1.0 - np.abs((fine[:, None] + 0.5) / RATIO - 0.5 - coarse[None, :]))


def sign(odd, mirrored):
    return -1.0 if (odd and mirrored) else 1.0


def swap_pairs(count):
    first, second = np.triu_indices(count)
    above, beyond = np.triu_indices(count, 1)
    return (first, second), (above, beyond)


def dense_table():
    spectra = line_spectra(HOCK, 36, 1)
    target = np.arange(20)[None, :] - RATIO
    source = np.arange(16)[:, None]
    near, far = np.abs(target - source), np.abs(target - (PATCH - 1 - source))

    def pick(first, second):
        return spectra[:, first[:, None, :, None], second[None, :, None, :]]

    terms = {(a, b): pick((near, far)[a], (near, far)[b]) for a in (0, 1) for b in (0, 1)}
    table = np.zeros((NF, ROWS, 256))
    for parity in range(4):
        odd_z, odd_x = divmod(parity, 2)
        if parity == 2:
            continue
        total = sum(sign(odd_z, a) * sign(odd_x, b) * terms[a, b] for a in (0, 1) for b in (0, 1))
        total = 0.25 * total
        if parity == 1:
            flat = total.reshape(NF, 256, 400)
            table[:, 544:800] = flat[:, :, :256]
            table[:, 800:1056, :144] = flat[:, :, 256:]
            continue
        base = 0 if parity == 0 else 272
        whole_in, strict_in = swap_pairs(16)
        whole_out, strict_out = swap_pairs(20)
        swapped = total.transpose(0, 2, 1, 3, 4)
        both, less = 0.5 * (total + swapped), 0.5 * (total - swapped)
        table[:, base : base + 136, :210] = both[:, whole_in[0], whole_in[1]][
            :, :, whole_out[0], whole_out[1]
        ]
        table[:, base + 144 : base + 264, :190] = less[:, strict_in[0], strict_in[1]][
            :, :, strict_out[0], strict_out[1]
        ]
    result = np.empty((NF, 2, ROWS, 256), ml_dtypes.bfloat16)
    result[:, 0], result[:, 1] = halves(table)
    return result


def swap_tables():
    whole, strict = swap_pairs(16)
    inward = np.zeros((16, 16, 384))
    spots = np.arange(136)
    inward[whole[0], whole[1], spots] = 1.0
    inward[whole[1], whole[0], spots] = 1.0
    spots = 256 + np.arange(120)
    inward[strict[0], strict[1], spots] = 1.0
    inward[strict[1], strict[0], spots] = -1.0
    whole, strict = swap_pairs(20)
    outward = np.zeros((2, 512, 20, 20))
    spots = np.arange(210)
    outward[0, spots, whole[0], whole[1]] = 1.0
    outward[0, spots, whole[1], whole[0]] = 1.0
    spots = 256 + np.arange(190)
    outward[0, spots, strict[0], strict[1]] = 1.0
    outward[0, spots, strict[1], strict[0]] = -1.0
    outward[1, :400] = np.eye(400).reshape(20, 20, 20, 20).transpose(1, 0, 2, 3).reshape(400, 20, 20)
    turn = np.eye(256).reshape(16, 16, 16, 16).transpose(1, 0, 2, 3).reshape(256, 256)
    return tuple(
        table.astype(ml_dtypes.bfloat16)
        for table in (inward.reshape(256, 384), turn, outward.reshape(2, 512, 400))
    )


def coarse_dense_table():
    spectra = line_spectra(CH, 10, RATIO)
    window = np.arange(-2, CQ + 2)
    apart = np.abs(window[:, None] - np.arange(CQ)[None, :])
    kernel = spectra[:, apart[:, None, :, None], apart[None, :, None, :]]
    spread = refine_table(np.arange(20) - RATIO, window)
    kernel = np.einsum("za,xb,fabcd->fcdzx", spread, spread, kernel)
    whole, strict = swap_pairs(20)
    result = np.empty((NC, 4, 2, 16, 512), ml_dtypes.bfloat16)
    for parity in range(4):
        odd_z, odd_x = divmod(parity, 2)
        mirrored = kernel[:, ::-1]
        total = kernel + (-1.0) ** odd_z * mirrored
        total = total + (-1.0) ** odd_x * total[:, :, ::-1]
        total = 0.25 * total[:, :4, :4].reshape(NC, 16, 20, 20)
        swapped = total.transpose(0, 1, 3, 2)
        table = np.zeros((NC, 16, 512))
        if parity == 1:
            table[:, :, :400] = total.reshape(NC, 16, 400)
        elif parity == 2:
            table[:, :, :400] = swapped.reshape(NC, 16, 400)
        else:
            table[:, :, :210] = (0.5 * (total + swapped))[:, :, whole[0], whole[1]]
            table[:, :, 256:446] = (0.5 * (total - swapped))[:, :, strict[0], strict[1]]
        result[:, parity, 0], result[:, parity, 1] = halves(table)
    return result


def forward_table():
    cells = np.arange(PATCH)
    lines = np.zeros((NG, 2, PATCH))
    lines[:NF] = fine_basis(cells)
    lines[NF : NF + NC] = coarse_basis(cells // RATIO)
    table = np.zeros((NG, 2, 4, 4, PATCH))
    for patch in range(4):
        table[:, :, patch, patch] = lines
    high, low = halves(table.reshape(4, 96, 128))
    return np.concatenate([high, low], axis=1)


def mirror_table():
    table = np.zeros((64, 128))
    for patch in range(4):
        for cell in range(16):
            table[patch * 16 + cell, patch * 32 + 31 - cell] = 1.0
    return table.astype(ml_dtypes.bfloat16)


def gather_table():
    table = np.zeros((16, 16, 4, 4))
    for z in range(16):
        for x in range(16):
            table[z, x, z // RATIO, x // RATIO] = 1.0
    return table.reshape(256, 16).astype(ml_dtypes.bfloat16)


def alias_weights():
    fine = np.arange(HOCK)
    spread = np.zeros((HOCK, CH))
    for shift in (-1, 0, 1):
        spread += refine_table(fine, np.arange(CH) + shift * CH)
    mapped = np.einsum("fct,tY,GcY->fcG", fine_basis(fine), spread, coarse_basis(np.arange(CH)))
    rest = np.arange(NF) % CH
    alias = np.minimum(rest, CH - rest)
    return mapped[np.arange(NF), :, alias]


BLOCK = 128
BEYOND = [128, 129, 130, 131, -4, -3, -2, -1]
UPPER = [128, 129, 130, 131, 124, 125, 126, 127]
LOWER = [0, 1, 2, 3, -4, -3, -2, -1]
PLACES = np.array(list(range(BLOCK)) + BEYOND + UPPER + LOWER)


def backward_table():
    table = np.zeros((160, 38, 2, 4))
    for patch in range(4):
        cells = PLACES - PATCH * patch
        inside = (cells >= -RATIO) & (cells < PATCH + RATIO)
        values = fine_basis(cells) * inside
        table[:152, :NF, :, patch] = values.transpose(2, 0, 1)
    high, low = halves(table.reshape(160, 304))
    return np.concatenate([high, high, low], axis=1)


def unfold_table():
    table = np.zeros((2, 2, 160, 2, 4, 2, 20))
    for odd in range(2):
        for patch in range(4):
            for row, place in enumerate(PLACES):
                cell = place - PATCH * patch + RATIO
                if 0 <= cell < 20:
                    column, value = cell, 1.0
                elif 20 <= cell < 40:
                    column, value = 39 - cell, sign(odd, 1)
                else:
                    continue
                for layer in range(2):
                    table[0, layer, row, odd, patch, layer, column] = value
                    table[1, layer, row, odd, patch, 1 - layer, column] = value
    return table.reshape(2, PAIRS, 320).astype(ml_dtypes.bfloat16)


def periodic_basis(length, cells):
    slots = np.arange(length)
    freq = np.where(slots <= length // 2, slots, slots - length // 2)
    weight = np.where((freq == 0) | (freq == length // 2), 1.0, 2.0)
    angle = 2.0 * math.pi / length * (freq[:, None] * cells[None, :] % length)
    basis = np.where((slots <= length // 2)[:, None], np.cos(angle), np.sin(angle))
    return basis * np.sqrt(weight / length)[:, None], freq


REACH = CQ + 2
SIDE = 34
LANES = 384


def far_tables(total_z, total_x, total_y, parts_x, parts_y):
    basis_y, freq_y = periodic_basis(total_y, np.arange(total_y))
    basis_x, freq_x = periodic_basis(total_x, np.arange(total_x))
    along_y = np.zeros((parts_y, 4, 32, 4, total_y))
    for layer in range(4):
        along_y[:, layer, :, layer, :] = basis_y.T.reshape(parts_y, 32, total_y)
    along_y = np.stack(halves(along_y.reshape(parts_y, 128, 4 * total_y)), axis=1)
    high, low = halves(basis_x.reshape(total_x, parts_x, 32).transpose(1, 0, 2))
    along_x = np.concatenate([high, high, low], axis=2)

    def eigen(freq, length):
        return 2.0 - 2.0 * np.cos(2.0 * math.pi / length * freq)

    freq_z = np.arange(total_z)
    square = (
        eigen(freq_z, total_z)[:, None, None]
        + eigen(freq_x, total_x)[None, :, None]
        + eigen(freq_y, total_y)[None, None, :]
    )
    square[0, 0, 0] = 1.0
    inverse = 1.0 / (RATIO * square)
    inverse[0, 0, 0] = 0.0
    steps = np.arange(total_z // 2 + 1)
    cosine = np.cos(2.0 * math.pi / total_z * np.outer(steps, freq_z)) / total_z
    column = np.einsum("dk,kxy->dxy", cosine, inverse).astype(np.float32)

    def windows(length, parts, basis):
        table = np.zeros((parts, 40, length))
        for part in range(parts):
            cells = (np.arange(SIDE) - 1 + part * 32) % length
            table[part, :SIDE] = basis[:, cells].T
        return table.reshape(parts * 40, length)

    square = eigen(freq_x, total_x)[:, None] + eigen(freq_y, total_y)[None, :]
    square[0, 0] = 1.0
    inverse = 1.0 / (RATIO * square)
    inverse[0, 0] = 0.0
    weight = np.outer(basis_x[:, :32].sum(axis=1), basis_y[:, :32].sum(axis=1)) * inverse
    flat = basis_x.T @ weight @ basis_y
    even = np.zeros((parts_x, parts_y, 40, LANES))
    for part in range(parts_x):
        cells_x = (np.arange(SIDE) - 1 + part * 32) % total_x
        for other in range(parts_y):
            cells_y = (np.arange(SIDE) - 1 + other * 32) % total_y
            values = flat[cells_x][:, cells_y].T
            even[part, other, :SIDE, : REACH * SIDE] = np.tile(values, (1, REACH))
    even = even.reshape(parts_x * parts_y, 40, LANES).astype(np.float32)

    back_x = np.concatenate(halves(windows(total_x, parts_x, basis_x)), axis=1)
    back_y = np.stack(halves(windows(total_y, parts_y, basis_y)))
    return along_y, along_x, column, back_x, back_y, even


def parts_of(values):
    high = values.astype(b16)
    return high, (values - high.astype(f32)).astype(b16)


def mul(left, right):
    return jnp.dot(left, right, preferred_element_type=f32)


def mul_nt(left, right):
    return lax.dot_general(left, right, (((1,), (1,)), ((), ())), preferred_element_type=f32)


def masses_kernel(rho_ref, out_ref):
    row = lax.broadcasted_iota(jnp.int32, (32, 512), 0)
    column = lax.broadcasted_iota(jnp.int32, (32, 512), 1)
    sum_x = jnp.where(column % 128 // RATIO == row, 1.0, 0.0).astype(b16)
    row = lax.broadcasted_iota(jnp.int32, (128, 128), 0)
    column = lax.broadcasted_iota(jnp.int32, (128, 128), 1)
    for half in range(2):
        total = jnp.zeros((32, 128), f32)
        for layer in range(4):
            z = (half * 4 + layer) * RATIO
            slab = rho_ref[pl.ds(z, RATIO)].reshape(RATIO * 128, 128)
            rows = mul(sum_x, slab)
            high, rest = parts_of(rows)
            mid, low = parts_of(rows - high.astype(f32))
            weights = jnp.where(row // RATIO + layer * 32 == column, 1.0, 0.0).astype(b16)
            total += mul(high, weights) + (mul(mid, weights) + mul(low, weights))
        for copy in range(out_ref.shape[0]):
            out_ref[copy, half * 32 : half * 32 + 32, :] = total


def mul_pairs(values, high_table, low_table):
    rows = values.shape[0]
    high, low = parts_of(values)
    both = mul(jnp.concatenate([high, low], axis=0), high_table)
    return both[:rows] + (both[rows:] + mul(high, low_table))


def mul_exact(values, table):
    rows = values.shape[0]
    high, low = parts_of(values)
    both = mul(jnp.concatenate([high, low], axis=0), table)
    return both[:rows] + both[rows:]


def near_kernel(
    weights_ref,
    rho_ref,
    forward_ref,
    mirror_ref,
    gather_ref,
    coarse_ref,
    backward_ref,
    inward_ref,
    turn_ref,
    outward_ref,
    dense_ref,
    wide_ref,
    upper_ref,
    lower_ref,
    bottom_ref,
    top_ref,
    lines,
    ready,
    smooth,
    spectra,
    turned,
    ring,
    arrived,
):
    def fetch(freq, slot):
        return pltpu.make_async_copy(dense_ref.at[freq], ring.at[slot], arrived.at[slot])

    for slot in range(RING):
        fetch(slot, slot).start()

    for z in range(PATCH):
        turned[z] = mul(mirror_ref[...], rho_ref[z]).astype(b16)
    for patch in range(4):
        def rows(mirror_z, mirror_x):
            tiles = []
            for z in range(16):
                layer = PATCH - 1 - z if mirror_z else z
                if mirror_x:
                    tiles.append(turned[layer, patch * 16 : patch * 16 + 16, :])
                else:
                    tiles.append(rho_ref[layer, patch * 32 : patch * 32 + 16, :])
            return jnp.concatenate(tiles, axis=0)

        right = [rows(0, 0), rows(0, 1), rows(1, 0), rows(1, 1)]

        def chunk(index):
            left = forward_ref[index]
            sums = []
            for mirror in range(4):
                both = mul_nt(left, right[mirror])
                sums.append(both[:96] + both[96:])
            even, odd = sums[0] + sums[1], sums[0] - sums[1]
            even_far, odd_far = sums[2] + sums[3], sums[2] - sums[3]
            freqs = slice(index * 12, index * 12 + 12)
            lines[freqs, 0, patch] = (even + even_far).reshape(12, 8, 256)
            lines[freqs, 1, patch] = (odd + odd_far).reshape(12, 8, 256)
            lines[freqs, 2, patch] = (even - even_far).reshape(12, 8, 256)
            lines[freqs, 3, patch] = (odd - odd_far).reshape(12, 8, 256)

        for index in range(4):
            chunk(index)

    for parity in range(4):
        values = lines[NF : NF + NC, parity].reshape(NC * 32, 256)
        high, low = parts_of(mul_exact(values, gather_ref[...]))
        for freq in range(NC):
            both = jnp.concatenate(
                [high[freq * 32 : freq * 32 + 32], low[freq * 32 : freq * 32 + 32]], axis=0
            )
            value = mul(both, coarse_ref[freq, parity, 0])
            smooth[freq, parity] = value[:32] + (
                value[32:] + mul(both[:32], coarse_ref[freq, parity, 1])
            )

    def prepare(index):
        freqs = pl.ds(index * 4, 4)
        for slot, parity in ((0, 0), (1, 3)):
            values = lines[freqs, parity].reshape(128, 256)
            ready[freqs, slot] = mul_exact(values, inward_ref[...]).reshape(4, 32, 384)
        values = lines[freqs, 2].reshape(128, 256)
        ready[freqs, 2, :, 0:256] = mul_exact(values, turn_ref[...]).reshape(4, 32, 256)

    for index in range(NR // 4):
        prepare(index)
    spectra[:, :, 8 * NF :, :] = jnp.zeros((4, 4, 8, 512), f32)
    row = lax.broadcasted_iota(jnp.int32, (32, 1), 0)

    def solve(freq):
        slot = lax.rem(freq, RING)
        fetch(freq, slot).wait()
        rest = lax.rem(freq, CH)
        alias = jnp.minimum(rest, CH - rest)
        weight = jnp.where(row % 8 < 4, weights_ref[freq, 0], weights_ref[freq, 1])
        here = pl.ds(freq * 8, 8)

        def keep(parity, low, high, value):
            value = value - weight * smooth[alias, parity, :, low:high]
            spectra[parity, :, here, low:high] = value.reshape(4, 8, 256)

        for place, parity in ((0, 0), (1, 3)):
            for base, count, lane in ((0, 144, 0), (144, 128, 256)):
                base = base + 272 * place
                value = mul_pairs(
                    ready[freq, place, :, lane : lane + count],
                    ring[slot, 0, base : base + count, :],
                    ring[slot, 1, base : base + count, :],
                )
                keep(parity, lane, lane + 256, value)
        values = jnp.concatenate(
            [lines[freq, 1].reshape(32, 256), ready[freq, 2, :, 0:256]], axis=0
        )
        for base, lane in ((544, 0), (800, 256)):
            value = mul_pairs(
                values, ring[slot, 0, base : base + 256, :], ring[slot, 1, base : base + 256, :]
            )
            keep(1, lane, lane + 256, value[:32])
            keep(2, lane, lane + 256, value[32:])

        @pl.when(freq + RING < NF)
        def _():
            fetch(freq + RING, slot).start()

    def solve_some(index, carry):
        for part in range(4):
            solve(4 * index + part)
        return carry

    lax.fori_loop(0, NF // 4, solve_some, 0)
    solve(jnp.int32(NF - 1))

    for parity in range(4):
        values = []
        for patch in range(4):
            high, low = parts_of(spectra[parity, patch])
            values.append(mul(backward_ref[...], jnp.concatenate([high, low, high], axis=0)))
        if parity != 1:
            pairs = [part for value in values for part in parts_of(value)]
            table = outward_ref[1 if parity == 2 else 0]
            both = mul(jnp.concatenate(pairs, axis=0), table)
            values = [
                both[320 * patch : 320 * patch + 160] + both[320 * patch + 160 : 320 * patch + 320]
                for patch in range(4)
            ]
        for patch in range(4):
            wide_ref[parity, patch] = values[patch][:136, :400]
            upper_ref[parity, patch] = values[patch][136:144, :400]
            lower_ref[parity, patch] = values[patch][144:152, :400]

    for odd_x in range(2):
        for patch in range(4):
            index = odd_x * 4 + patch
            even = wide_ref[odd_x, patch, :, 0:128]
            odd = wide_ref[2 + odd_x, patch, :, 0:128]
            bottom_ref[index] = even + odd
            top_ref[index] = even - odd


def with_neighbours(values, from_lower, from_upper):
    first = lax.broadcasted_iota(jnp.int32, from_lower.shape, 0) < 4
    zero = jnp.zeros_like(from_lower)
    return jnp.concatenate(
        [
            values[0:8] + jnp.where(first, from_lower, zero),
            values[8:120],
            values[120:128] + jnp.where(first, zero, from_upper),
            values[128:136] + jnp.where(first, from_upper, from_lower),
        ],
        axis=0,
    )


def turned_into(ref, side, index, value):
    ref[side, index, :, 0:128] = value[:128].T
    ref[side, index, :, 128:136] = value[128:136].T


def rows_of(ref, side, pair):
    rows = slice(40 * pair, 40 * pair + 40)
    return jnp.concatenate([ref[side, index, rows, :] for index in range(8)], axis=0)


def unfolded(table, rows):
    high, low = parts_of(rows)
    return mul(table, high) + mul(table, low)


def store_layers(value, places, near_ref, upper_ref, lower_ref):
    for layer, z in enumerate(places):
        near_ref[z] = value[160 * layer : 160 * layer + 136]
        upper_ref[z] = value[160 * layer + 136 : 160 * layer + 144]
        lower_ref[z] = value[160 * layer + 144 : 160 * layer + 152]


def inner_kernel(
    wide_hbm,
    from_lower_hbm,
    from_upper_hbm,
    unfold_ref,
    near_hbm,
    upper_ref,
    lower_ref,
    outer_hbm,
    standing,
    wide_ref,
    from_lower_ref,
    from_upper_ref,
    near_ref,
    arrived,
    written,
):
    def fetch(index):
        return pltpu.make_async_copy(wide_hbm.at[:, index], wide_ref.at[:, index], arrived.at[index])

    strips = [
        pltpu.make_async_copy(from_lower_hbm, from_lower_ref, arrived.at[8]),
        pltpu.make_async_copy(from_upper_hbm, from_upper_ref, arrived.at[9]),
    ]
    for strip in strips:
        strip.start()
    for index in range(8):
        fetch(index).start()
    for strip in strips:
        strip.wait()

    def turn(index):
        fetch(index).wait()
        even = with_neighbours(wide_ref[0, index], from_lower_ref[0, index], from_upper_ref[0, index])
        odd = with_neighbours(wide_ref[1, index], from_lower_ref[1, index], from_upper_ref[1, index])
        turned_into(standing, 0, index, even + odd)
        turned_into(standing, 1, index, even - odd)

    for index in range(8):
        turn(index)
    results = [pltpu.make_async_copy(standing.at[:, :, 40:160, :], outer_hbm, written.at[0])]
    results[0].start()
    for pair in range(4, 10):
        for side in range(2):
            value = unfolded(unfold_ref[0], rows_of(standing, side, pair))
            places = [2 * pair - 8, 2 * pair - 7]
            if side == 1:
                places = [23 - z for z in places]
            store_layers(value, places, near_ref, upper_ref, lower_ref)
            pieces = pl.ds(min(places), 2)
            results.append(
                pltpu.make_async_copy(
                    near_ref.at[pieces], near_hbm.at[pieces], written.at[len(results)]
                )
            )
            results[-1].start()
    for result in results:
        result.wait()


def outer_kernel(
    outer_ref,
    from_below_ref,
    from_above_ref,
    corner_lower_ref,
    corner_upper_ref,
    unfold_ref,
    near_ref,
    upper_ref,
    lower_ref,
    given,
):
    def turn(index, carry):
        for side, ref in ((0, from_below_ref), (1, from_above_ref)):
            value = with_neighbours(
                ref[index], corner_lower_ref[side, index], corner_upper_ref[side, index]
            )
            turned_into(given, side, index, value)
        return carry

    lax.fori_loop(0, 8, turn, 0)
    for pair in range(3):
        for side in range(2):
            value = unfolded(unfold_ref[0], rows_of(outer_ref, side, pair))
            value = value + unfolded(unfold_ref[1], rows_of(given, side, 2 - pair))
            places = [2 * pair, 2 * pair + 1]
            if side == 1:
                places = [11 - z for z in places]
            store_layers(value, places, near_ref, upper_ref, lower_ref)


def far_kernel(
    where_ref,
    masses_ref,
    along_y_ref,
    along_x_ref,
    column_hbm,
    back_x_ref,
    back_y_ref,
    even_hbm,
    out_ref,
    spectra,
    lines,
    turned,
    column_ref,
    even_ref,
    arrived,
):
    tables = [
        pltpu.make_async_copy(column_hbm, column_ref, arrived.at[0]),
        pltpu.make_async_copy(even_hbm, even_ref, arrived.at[1]),
    ]
    for table in tables:
        table.start()
    blocks = masses_ref.shape[0]
    total = spectra.shape[0]
    masses = masses_ref[...].reshape(blocks * 64, 128)
    mean = jnp.sum(masses, axis=(0, 1), keepdims=True) * (1.0 / masses.size)
    high, low = parts_of(masses - mean)
    value = mul(high, along_y_ref[0, 0]) + (
        mul(low, along_y_ref[0, 0]) + mul(high, along_y_ref[0, 1])
    )
    high, low = parts_of(value)
    for half in range(2 * blocks):
        rows = slice(half * 32, half * 32 + 32)
        right = jnp.concatenate([high[rows], low[rows], high[rows]], axis=0)
        value = mul(along_x_ref[0], right)
        for layer in range(4):
            spectra[half * 4 + layer] = value[:, layer * 128 : layer * 128 + 128]

    start = where_ref[2] * CQ
    for table in tables:
        table.wait()

    def solve(tile, carry):
        rows = pl.ds(pl.multiple_of(tile * 8, 8), 8)
        sums = [jnp.zeros((8, 128), f32) for _ in range(REACH)]
        for step in range(total):
            value = spectra[lax.rem(start + step, total), rows, :]
            for layer in range(REACH):
                apart = abs(step - (layer - 1)) % total
                sums[layer] += value * column_ref[min(apart, total - apart), rows, :]
        for layer in range(REACH):
            lines[layer, rows, :] = sums[layer]
        return carry

    lax.fori_loop(0, 16, solve, 0)

    turned[:, REACH * SIDE :, :] = jnp.zeros((4, LANES - REACH * SIDE, 128), f32)
    for layer in range(REACH):
        high, low = parts_of(lines[layer])
        value = mul(back_x_ref[:, 0:128], high) + (
            mul(back_x_ref[:, 0:128], low) + mul(back_x_ref[:, 128:256], high)
        )
        for part in range(4):
            turned[part, layer * SIDE : layer * SIDE + SIDE, :] = value[part * 40 : part * 40 + SIDE]
    for part in range(4):
        high, low = parts_of(turned[part])
        value = mul_nt(back_y_ref[0], high) + (
            mul_nt(back_y_ref[0], low) + mul_nt(back_y_ref[1], high)
        )
        for other in range(4):
            apart = lax.rem(part + 4 - where_ref[0], 4) * 4 + lax.rem(other + 4 - where_ref[1], 4)
            out_ref[part * 4 + other] = value[other * 40 : other * 40 + 40] + mean * even_ref[apart]


def share(fine, coarse):
    fine = jnp.where(fine < 132, fine, fine - 136).astype(f32)
    return jnp.maximum(0.0, 1.0 - jnp.abs((fine + 0.5) / RATIO - 0.5 - coarse.astype(f32)))


def planes_kernel(far_ref, out_ref):
    sums = far_ref[0]
    for source in range(1, far_ref.shape[0]):
        sums = sums + far_ref[source]
    right = jnp.concatenate(parts_of(sums), axis=0)
    row = lax.broadcasted_iota(jnp.int32, (136, LANES), 0)
    lane = lax.broadcasted_iota(jnp.int32, (136, LANES), 1)
    spread_x = []
    for layer in range(REACH):
        coarse = lane - layer * SIDE
        inside = (coarse >= 0) & (coarse < SIDE)
        spread_x.append(jnp.where(inside, share(row, coarse - 1), 0.0).astype(b16))
    value = mul_nt(jnp.concatenate(spread_x, axis=0), right)
    first, second = parts_of(value[:, :40] + value[:, 40:])
    row = lax.broadcasted_iota(jnp.int32, (40, 256), 0)
    lane = lax.broadcasted_iota(jnp.int32, (40, 256), 1)
    spread_y = jnp.where(row < SIDE, share(lane, row - 1), 0.0).astype(b16)
    value = mul(first, spread_y) + mul(second, spread_y)
    for layer in range(REACH):
        out_ref[layer] = value[layer * 136 : layer * 136 + 136]


def final_kernel(
    inner_ref,
    inner_lower_ref,
    inner_upper_ref,
    outer_ref,
    outer_lower_ref,
    outer_upper_ref,
    planes_ref,
    potential_ref,
    force_ref,
    whole,
    depth,
):
    step = pl.program_id(0)

    @pl.when(step == 0)
    def _():
        for z in range(36):
            place = (z - 2 + 0.5) / RATIO - 0.5
            below = math.floor(place)
            part = place - below
            if 6 <= z < 30:
                refs, spot = (inner_ref, inner_lower_ref, inner_upper_ref), z - 6
            else:
                refs, spot = (outer_ref, outer_lower_ref, outer_upper_ref), z % 24
            value = with_neighbours(*(ref[spot] for ref in refs))
            whole[z] = value + (
                (1.0 - part) * planes_ref[below + 1] + part * planes_ref[below + 2]
            )

    row = lax.broadcasted_iota(jnp.int32, (128, 128), 0)
    lane = lax.broadcasted_iota(jnp.int32, (128, 128), 1)

    def difference(plus_one, minus_one, plus_two, minus_two):
        value = -(2.0 / 3.0 * (plus_one - minus_one) - 1.0 / 12.0 * (plus_two - minus_two))
        return value.astype(b16)

    def beyond(values, edge, mask, shift, axis):
        return pltpu.roll(jnp.where(mask, edge, values), shift, axis)

    for inner in range(depth):
        z = step * depth + inner + 2
        here = whole[z, 0:128, 0:128]
        potential_ref[inner] = here
        force_ref[0, inner] = difference(
            whole[z + 1, 0:128, 0:128],
            whole[z - 1, 0:128, 0:128],
            whole[z + 2, 0:128, 0:128],
            whole[z - 2, 0:128, 0:128],
        )
        edge = whole[z, 128:136, 0:128]
        above = jnp.concatenate([edge, here[8:]], axis=0)
        below = jnp.concatenate([here[:120], edge], axis=0)
        force_ref[1, inner] = difference(
            beyond(here, above, row < 1, 127, 0),
            beyond(here, below, row >= 127, 1, 0),
            beyond(here, above, row < 2, 126, 0),
            beyond(here, below, row >= 126, 2, 0),
        )
        above = whole[z, 0:128, 128:256]
        below = pltpu.roll(above, 120, 1)
        force_ref[2, inner] = difference(
            beyond(here, above, lane < 1, 127, 1),
            beyond(here, below, lane >= 127, 1, 1),
            beyond(here, above, lane < 2, 126, 1),
            beyond(here, below, lane >= 126, 2, 1),
        )


VMEM = pl.BlockSpec(memory_space=pltpu.VMEM)
HBM = pl.BlockSpec(memory_space=pltpu.HBM)
SMEM = pl.BlockSpec(memory_space=pltpu.SMEM)


def params(size):
    return pltpu.CompilerParams(vmem_limit_bytes=size * MIB)


def cost(flops, moved):
    return pl.CostEstimate(flops=int(flops), bytes_accessed=int(moved), transcendentals=0)


def shape(*dims, dtype=f32):
    return jax.ShapeDtypeStruct(dims, dtype)


def make_tables(size_z, size_x, size_y):
    return dict(
        weights=alias_weights().astype(np.float32),
        forward=forward_table(),
        mirror=mirror_table(),
        gather=gather_table(),
        coarse=coarse_dense_table(),
        backward=backward_table(),
        dense=dense_table(),
        swap=swap_tables(),
        unfold=unfold_table(),
        far=far_tables(size_z * CQ, size_x * 32, size_y * 32, size_x, size_y),
    )


def masses_of(density, copies):
    return pl.pallas_call(
        masses_kernel,
        out_shape=shape(copies, 64, 128),
        in_specs=[VMEM],
        out_specs=VMEM,
        compiler_params=params(16),
        cost_estimate=cost(2e7, 1.2e6),
        name="masses",
    )(density)


def near_of(density, tables):
    strip = shape(4, 4, 8, 400)
    face = shape(8, 136, 128)
    return pl.pallas_call(
        near_kernel,
        out_shape=(shape(4, 4, 136, 400), strip, strip, face, face),
        in_specs=[SMEM] + [VMEM] * 9 + [pl.BlockSpec(memory_space=pl.ANY)],
        out_specs=(VMEM,) * 5,
        scratch_shapes=[
            pltpu.VMEM((NG, 4, 4, 8, 256), f32),
            pltpu.VMEM((NR, 3, 32, 384), f32),
            pltpu.VMEM((NC, 4, 32, 512), f32),
            pltpu.VMEM((4, 4, 304, 512), f32),
            pltpu.VMEM((PATCH, 64, 128), b16),
            pltpu.VMEM((RING, 2, ROWS, 256), b16),
            pltpu.SemaphoreType.DMA((RING,)),
        ],
        compiler_params=params(54),
        cost_estimate=cost(8e9, 5e7),
        name="near",
    )(
        tables["weights"],
        density,
        tables["forward"],
        tables["mirror"],
        tables["gather"],
        tables["coarse"],
        tables["backward"],
        *tables["swap"],
        tables["dense"],
    )


def inner_of(wide, from_lower, from_upper, tables):
    return pl.pallas_call(
        inner_kernel,
        out_shape=(
            shape(24, 136, 256),
            shape(24, 8, 256),
            shape(24, 8, 256),
            shape(2, 8, 120, 256),
        ),
        in_specs=[HBM] * 3 + [VMEM],
        out_specs=(HBM, VMEM, VMEM, HBM),
        scratch_shapes=[
            pltpu.VMEM((2, 8, 400, 256), f32),
            pltpu.VMEM((2, 8, 136, 400), f32),
            pltpu.VMEM((2, 8, 8, 400), f32),
            pltpu.VMEM((2, 8, 8, 400), f32),
            pltpu.VMEM((24, 136, 256), f32),
            pltpu.SemaphoreType.DMA((10,)),
            pltpu.SemaphoreType.DMA((13,)),
        ],
        compiler_params=params(60),
        cost_estimate=cost(5e9, 1e7),
        name="inner",
    )(wide, from_lower, from_upper, tables["unfold"])


def outer_of(outer, from_below, from_above, corner_lower, corner_upper, tables):
    return pl.pallas_call(
        outer_kernel,
        out_shape=(shape(12, 136, 256), shape(12, 8, 256), shape(12, 8, 256)),
        in_specs=[VMEM] * 6,
        out_specs=(VMEM,) * 3,
        scratch_shapes=[pltpu.VMEM((2, 8, 128, 256), f32)],
        compiler_params=params(16),
        cost_estimate=cost(4e9, 5e6),
        name="outer",
    )(outer, from_below, from_above, corner_lower, corner_upper, tables["unfold"])


def planes_of(far):
    return pl.pallas_call(
        planes_kernel,
        out_shape=shape(REACH, 136, 256),
        in_specs=[VMEM],
        out_specs=VMEM,
        compiler_params=params(12),
        cost_estimate=cost(3e9, 2e6),
        name="planes",
    )(far)


def far_of(where, masses, tables):
    along_y, along_x, column, back_x, back_y, even = tables["far"]
    parts = along_x.shape[0] * along_y.shape[0]
    total = masses.shape[0] * CQ

    def fixed(*dims):
        return pl.BlockSpec(dims, lambda i, w: (0,) * len(dims))

    return pl.pallas_call(
        far_kernel,
        grid_spec=pltpu.PrefetchScalarGridSpec(
            num_scalar_prefetch=1,
            grid=(1,),
            in_specs=[
                fixed(*masses.shape),
                pl.BlockSpec((1, 2, 128, 512), lambda i, w: (w[1], 0, 0, 0)),
                pl.BlockSpec((1, 128, 96), lambda i, w: (w[0], 0, 0)),
                HBM,
                fixed(*back_x.shape),
                fixed(*back_y.shape),
                HBM,
            ],
            out_specs=fixed(parts, 40, LANES),
            scratch_shapes=[
                pltpu.VMEM((total, 128, 128), f32),
                pltpu.VMEM((REACH, 128, 128), f32),
                pltpu.VMEM((4, LANES, 128), f32),
                pltpu.VMEM(column.shape, f32),
                pltpu.VMEM(even.shape, f32),
                pltpu.SemaphoreType.DMA((2,)),
            ],
        ),
        out_shape=shape(parts, 40, LANES),
        compiler_params=params(60),
        cost_estimate=cost(4e9, 9e6),
        name="far",
    )(where, masses, along_y, along_x, column, back_x, back_y, even)


def final_of(inner, outer, planes):
    depth = 4
    operands = (*inner, *outer, planes)
    return pl.pallas_call(
        functools.partial(final_kernel, depth=depth),
        grid=(PATCH // depth,),
        out_shape=(shape(PATCH, 128, 128), shape(3, PATCH, 128, 128, dtype=b16)),
        in_specs=[pl.BlockSpec(values.shape, lambda i: (0, 0, 0)) for values in operands],
        out_specs=(
            pl.BlockSpec((depth, 128, 128), lambda i: (i, 0, 0)),
            pl.BlockSpec((3, depth, 128, 128), lambda i: (0, i, 0, 0)),
        ),
        scratch_shapes=[pltpu.VMEM((36, 136, 256), f32)],
        compiler_params=params(26),
        cost_estimate=cost(2e8, 1.2e7),
        name="final",
    )(*operands)


def moved(values, **steps):
    axes = tuple(steps)
    sizes = [lax.axis_size(axis) for axis in axes]
    pairs = []
    for source in np.ndindex(*sizes):
        target = [(i + step) % size for i, step, size in zip(source, steps.values(), sizes)]
        pairs.append(
            (int(np.ravel_multi_index(source, sizes)), int(np.ravel_multi_index(target, sizes)))
        )
    return lax.ppermute(values, axes, pairs)


def body(tables, density):
    size_gz = lax.axis_size("gz")
    where = jnp.stack([lax.axis_index(axis) for axis in ("gx", "gy", "gz")]).astype(jnp.int32)
    masses = masses_of(density, size_gz)
    masses = lax.all_to_all(masses, "gz", 0, 0, tiled=True)
    wide, upper, lower, bottom, top = near_of(density, tables)
    from_below = moved(top, gz=1)
    from_above = moved(bottom, gz=-1)
    from_lower = moved(upper, gy=1).reshape(2, 8, 8, 400)
    from_upper = moved(lower, gy=-1).reshape(2, 8, 8, 400)
    far = far_of(where, masses, tables)
    far = lax.all_to_all(far, ("gx", "gy"), 0, 0, tiled=True)
    faces = jnp.stack([from_below, from_above])
    corner_lower = moved(jnp.concatenate([faces[:, :, 128:132], faces[:, :, 124:128]], axis=2), gy=1)
    corner_upper = moved(jnp.concatenate([faces[:, :, 0:4], faces[:, :, 132:136]], axis=2), gy=-1)
    wide = wide.reshape(2, 8, 136, 400)
    near, upper, lower, outer = inner_of(wide, from_lower, from_upper, tables)
    inner = (near, moved(upper, gx=1), moved(lower, gx=-1))
    near, upper, lower = outer_of(
        outer, from_below, from_above, corner_lower, corner_upper, tables
    )
    outer = (near, moved(upper, gx=1), moved(lower, gx=-1))
    return final_of(inner, outer, planes_of(far))


def solution(mesh):
    tables = make_tables(mesh.shape["gz"], mesh.shape["gx"], mesh.shape["gy"])
    return jax.shard_map(
        functools.partial(body, tables),
        mesh=mesh,
        in_specs=(P("gz", "gx", "gy"),),
        out_specs=(P("gz", "gx", "gy"), P(None, "gz", "gx", "gy")),
        check_vma=False,
    )
```
